512 devices in a mesh: inst: 32 (over z, x), tp: 16 (over y, core).
Axes of the slice: x: 4, y: 8, z: 8, core: 2. Of those that a mesh axis runs over, the one named last changes fastest.
Arguments:
- pool: bfloat16 [1280, 16, 2, 64, 128], P('inst', 'tp'), may hold values from -6 to 6
- sectioning: bfloat16 [1024, 16, 2, 64, 128], P('inst', 'tp'), may hold values from -6 to 6
- spill_to: int32 [1024], P('inst'), may hold values from 0 to 31, as said below
- tables: int32 [32, 111, 2], replicated, may hold values from -1 to 103, as said below
- lengths: int32 [32], replicated, may hold values from 4097 to 14208, as said below
- queries: bfloat16 [32, 4, 64, 128], P('inst', None, 'tp'), may hold values from -64 to 64
- new_kv: bfloat16 [32, 4, 2, 8, 128], P('inst'), may hold values from -6 to 6
Outputs:
- attended: bfloat16 [32, 4, 64, 128], P('inst', None, 'tp')
- lent: bfloat16 [2048, 16, 2, 64, 128], P('inst', 'tp')
The draws below stay inside these ranges and needn't reach their ends.
Inputs may be any that keep to these rules, and one draw needn't show every extreme that they name: `spill_to`: the sectioned pages of one instance go at most 2 times to the same instance (possibly itself); on every instance some destination receives exactly 2 of them. tables[r, n] = (instance, slot) holding page n of request r, and (-1, -1) beyond the request's pages. Slots below 40 are resident; slot 40 + i * 2 + k is the k-th page that instance i lends there, counted in sectioning order. Every resident slot holds exactly one page of some request; request r is owned by instance r, and its last 32 pages are that instance's sectioned pages in sectioning order. Request r has ceil(lengths[r] / 128) pages, all listed in tables.
All inputs are finite; a program needn't handle non-finite values.
Results may differ from the reference program's by a relative error of at most 0.0035.
Values may be sent and summed in bfloat16 or wider, within the bound.
No kernel may reach another device: no remote copies, remote signals or barrier semaphores. Data moves between devices by JAX's collectives and lax.ppermute only.
A program may use at most 128 MiB of HBM per device.

```python
import jax
import jax.numpy as jnp
from jax import lax

QH = 64
KVH = 8
HD = 128
PAGE = 128
STEPS = 4
CAP = 2
RES = 40
HALF = 64
KVL = 1
SECTION = 32
LENT = 64
REQUESTS = 32
MAXP = 111
N_INST = 32


def layout(key):
    sub_keys = jax.random.split(key, 6)
    inst_count = SECTION
    shuffles = jax.vmap(lambda single: jax.random.permutation(single, inst_count))(jax.random.split(sub_keys[0], inst_count))
    repeats = jax.random.randint(sub_keys[1], (inst_count,), 1, inst_count // 2 + 1)
    section_order = jnp.arange(inst_count, dtype=jnp.int32)
    cut_point = inst_count - repeats[:, None]
    picked = jnp.where(section_order[None, :] < cut_point, section_order[None, :], section_order[None, :] - cut_point)
    destination = jnp.take_along_axis(shuffles, picked, axis=1).astype(jnp.int32)
    same_dest = destination[:, :, None] == destination[:, None, :]
    earlier = section_order[None, :] < section_order[:, None]
    dest_rank = jnp.sum(jnp.where(same_dest & earlier[None], 1, 0), axis=2).astype(jnp.int32)
    average = RES
    pairing = jax.random.permutation(sub_keys[2], inst_count)
    shifts = jax.random.randint(sub_keys[3], (inst_count // 2,), 0, average).at[0].set(average - 1)
    counts = jnp.zeros((inst_count,), jnp.int32)
    counts = counts.at[pairing[0::2]].set(average - shifts).at[pairing[1::2]].set(average + shifts)
    slot_order = jax.random.permutation(sub_keys[4], inst_count * RES).astype(jnp.int32)
    first_slot = jnp.cumsum(counts) - counts
    page_number = jnp.arange(MAXP, dtype=jnp.int32)[None, :]
    resident = page_number < counts[:, None]
    global_slot = slot_order[jnp.clip(first_slot[:, None] + page_number, 0, inst_count * RES - 1)]
    sectioned_row = jnp.clip(page_number - counts[:, None], 0, SECTION - 1)
    sectioned = (page_number >= counts[:, None]) & (page_number < counts[:, None] + SECTION)
    owner_index = jnp.arange(inst_count, dtype=jnp.int32)[:, None]
    sectioned_holder = jnp.take_along_axis(destination, sectioned_row, axis=1)
    sectioned_slot = RES + owner_index * CAP + jnp.take_along_axis(dest_rank, sectioned_row, axis=1)
    holder = jnp.where(resident, global_slot // RES, jnp.where(sectioned, sectioned_holder, -1))
    slot_index = jnp.where(resident, global_slot % RES, jnp.where(sectioned, sectioned_slot, -1))
    tables = jnp.stack([holder, slot_index], axis=-1).astype(jnp.int32)
    last_fill = jax.random.randint(sub_keys[5], (inst_count,), 1, PAGE + 1)
    last_fill = last_fill.at[pairing[0]].set(1).at[pairing[1]].set(PAGE)
    lengths = ((counts + SECTION - 1) * PAGE + last_fill).astype(jnp.int32)
    return (destination.reshape(-1), tables, lengths)


def draw_spill_to(key, part):
    return layout(key)[0]


def draw_tables(key, part):
    return layout(key)[1]


def draw_lengths(key, part):
    return layout(key)[2]


def draw_queries(key, part):
    key = jax.random.fold_in(key, 11)
    first_key = jax.random.fold_in(key, 0)
    shape = (REQUESTS, STEPS, QH, HD)
    values = jax.random.normal(first_key, shape, jnp.float32) * 3.0
    return jnp.clip(values, -64.0, 64.0).astype(jnp.bfloat16)


def block_levels(rng, extent, cuts, low, high):
    loudness = 1.0
    for dim, blocks in cuts:
        draws = jax.random.uniform(jax.random.fold_in(jax.random.fold_in(rng, 6), dim), (blocks,), jnp.float32, low / len(cuts), high / len(cuts))
        loudness = loudness * jnp.repeat(jnp.exp(draws), extent[dim] // blocks).reshape((-1,) + (1,) * (len(extent) - 1 - dim))
    return loudness


def noise(own_key, shape, spread, bound, shards=(), kind=jnp.bfloat16):
    drawn = jax.random.normal(own_key, shape, jnp.float32) * spread
    if len(shards) > 0:
        drawn = block_levels(own_key, shape, shards, -0.22, 0.18) * drawn
    return jnp.clip(drawn, min=-bound, max=bound).astype(kind)


def setup_inputs(seed: int = 0) -> dict:
    splits = jax.random.split(jax.random.key(seed), 8)
    return {
        "pool": noise(splits[0], (N_INST * RES, 2 * KVH, 2, HALF, HD), 1.0, 6.0, ((0, 32), (1, 16))),
        "sectioning": noise(splits[1], (N_INST * SECTION, 2 * KVH, 2, HALF, HD), 1.0, 6.0, ((0, 32), (1, 16))),
        "spill_to": draw_spill_to(jax.random.fold_in(splits[7], 71), 0),
        "tables": draw_tables(jax.random.fold_in(splits[7], 71), 0),
        "lengths": draw_lengths(jax.random.fold_in(splits[7], 71), 0),
        "queries": draw_queries(jax.random.fold_in(splits[7], 71), 0),
        "new_kv": noise(splits[6], (REQUESTS, STEPS, 2, KVH, HD), 1.0, 6.0, ((0, 32),)),
    }


NEG = -1.0e30


def spill_rank(spill_to):
    destination = spill_to.reshape(N_INST, SECTION)
    section_order = jnp.arange(SECTION, dtype=jnp.int32)
    same_dest = destination[:, :, None] == destination[:, None, :]
    earlier = section_order[None, :] < section_order[:, None]
    return jnp.sum(jnp.where(same_dest & earlier[None], 1, 0), axis=2).astype(jnp.int32)


def reference(pool, sectioning, spill_to, tables, lengths, queries, new_kv):
    destination = spill_to.reshape(N_INST, SECTION)
    dest_rank = spill_rank(spill_to)
    source = jnp.arange(N_INST, dtype=jnp.int32)[:, None]
    flat_index = (destination * LENT + source * CAP + dest_rank).reshape(-1).astype(jnp.int32)
    lent_pages = jnp.zeros((N_INST * LENT,) + sectioning.shape[1:], sectioning.dtype).at[flat_index].set(sectioning)
    group_size = QH // KVH
    pair_count = KVH // KVL
    score_scale = HD ** -0.5
    blocks = MAXP * 2
    positions = jnp.arange(MAXP * PAGE, dtype=jnp.int32).reshape(blocks, HALF)
    step_order = jnp.arange(STEPS, dtype=jnp.int32)
    causal = step_order[None, :] <= step_order[:, None]

    def one_request(request):
        table_row = tables[request]
        holder = table_row[:, 0]
        slot_index = table_row[:, 1]
        from_pool = jnp.clip(holder * RES + slot_index, 0, N_INST * RES - 1).astype(jnp.int32)
        from_lent = jnp.clip(holder * LENT + slot_index - RES, 0, N_INST * LENT - 1).astype(jnp.int32)
        page_data = jnp.where((slot_index < RES)[:, None, None, None, None], pool[from_pool], lent_pages[from_lent])
        page_data = page_data.reshape(MAXP, pair_count, 2, KVL, 2, HALF, HD)
        page_data = jnp.transpose(page_data, (4, 1, 3, 0, 2, 5, 6)).reshape(2, KVH, blocks, HALF, HD)
        key_rows = page_data[0].astype(jnp.float32)
        value_rows = page_data[1].astype(jnp.float32)
        query_rows = queries[request].astype(jnp.float32).reshape(STEPS, KVH, group_size, HD)
        fresh_kv = new_kv[request].astype(jnp.float32)
        cached = jnp.einsum("skgd,kbtd->skgbt", query_rows, key_rows) * score_scale
        cached_mask = jnp.broadcast_to((positions < lengths[request])[None, None, None], cached.shape)
        cached_masked = jnp.where(cached_mask, cached, NEG)
        block_max = jnp.max(cached_masked, axis=4)
        block_weights = jnp.where(cached_mask, jnp.exp(cached_masked - block_max[..., None]), 0.0)
        block_sum = jnp.sum(block_weights, axis=4)
        block_rounded = lax.optimization_barrier(block_weights.astype(jnp.bfloat16)).astype(jnp.float32)
        block_mix = jnp.einsum("skgbt,kbtd->skgbd", block_rounded, value_rows)
        new_scores = jnp.einsum("skgd,jkd->skgj", query_rows, fresh_kv[:, 0]) * score_scale
        new_mask = jnp.broadcast_to(causal[:, None, None, :], new_scores.shape)
        new_masked = jnp.where(new_mask, new_scores, NEG)
        new_max = jnp.max(new_masked, axis=3)
        new_weights = jnp.where(new_mask, jnp.exp(new_masked - new_max[..., None]), 0.0)
        new_sum = jnp.sum(new_weights, axis=3)
        new_rounded = lax.optimization_barrier(new_weights.astype(jnp.bfloat16)).astype(jnp.float32)
        new_mix = jnp.einsum("skgj,jkd->skgd", new_rounded, fresh_kv[:, 1])
        row_max = jnp.maximum(jnp.max(block_max, axis=3), new_max)
        block_factor = jnp.exp(block_max - row_max[..., None])
        new_factor = jnp.exp(new_max - row_max)
        mixture = jnp.sum(block_mix * block_factor[..., None], axis=3) + new_mix * new_factor[..., None]
        norm_total = jnp.sum(block_sum * block_factor, axis=3) + new_sum * new_factor
        return (mixture / norm_total[..., None]).reshape(STEPS, QH, HD).astype(jnp.bfloat16)

    attended = lax.map(one_request, jnp.arange(REQUESTS, dtype=jnp.int32))
    return attended, lent_pages
```

```python
import functools

import jax
import jax.numpy as jnp
from jax import lax
from jax.experimental import pallas as pl
from jax.experimental.pallas import tpu as pltpu
from jax.sharding import Mesh, PartitionSpec as P

PAGE = 128
CAP = 2
NEG = -1e30
NT = (((1,), (1,)), ((), ()))


def pack_kernel(spill_ref, section_ref, query_ref, out_ref, zeros, spread, count, page_sems, query_sem):
    insts = out_ref.shape[0]
    sectioned, rows = section_ref.shape[0], section_ref.shape[1]
    spread[...] = jnp.broadcast_to(query_ref[...][None], spread.shape)
    query_copy = pltpu.make_async_copy(
        spread, out_ref.at[:, pl.ds(CAP * rows, query_ref.shape[0])], query_sem
    )
    query_copy.start()
    zeros[...] = jnp.zeros_like(zeros)

    def slot_copy(source, dest, rank):
        start = pl.multiple_of(rank * rows, rows)
        return pltpu.make_async_copy(
            source, out_ref.at[dest, pl.ds(start, rows)], page_sems.at[dest * CAP + rank]
        )

    for dest in range(insts):
        count[dest] = 0

    @pl.loop(0, sectioned)
    def _(row):
        dest = spill_ref[row]
        rank = count[dest]
        count[dest] = rank + 1
        slot_copy(section_ref.at[row], dest, rank).start()

    @pl.loop(0, insts)
    def _(dest):
        filled = count[dest]
        for rank in range(CAP):

            @pl.when(filled <= rank)
            def _():
                slot_copy(zeros, dest, rank).start()

    @pl.loop(0, insts)
    def _(dest):
        for rank in range(CAP):
            slot_copy(zeros, dest, rank).wait()

    query_copy.wait()


def pack(spill_to, section_pages, query_rows, insts):
    rows, head_dim = section_pages.shape[1:]
    query_count = query_rows.shape[0]
    return pl.pallas_call(
        pack_kernel,
        out_shape=jax.ShapeDtypeStruct((insts, CAP * rows + query_count, head_dim), section_pages.dtype),
        in_specs=[
            pl.BlockSpec(memory_space=pltpu.SMEM),
            pl.BlockSpec(memory_space=pl.ANY),
            pl.BlockSpec(memory_space=pltpu.VMEM),
        ],
        out_specs=pl.BlockSpec(memory_space=pl.ANY),
        scratch_shapes=[
            pltpu.VMEM((rows, head_dim), section_pages.dtype),
            pltpu.VMEM((insts, query_count, head_dim), query_rows.dtype),
            pltpu.SMEM((insts,), jnp.int32),
            pltpu.SemaphoreType.DMA((insts * CAP,)),
            pltpu.SemaphoreType.DMA,
        ],
        name="pack",
    )(spill_to, section_pages, query_rows)


def resident_kernel(score_scale, owner_ref, arrived_ref, kv_ref, out_ref, asked, score, top, total, mix, sem):
    requests, query_count = asked.shape[0], asked.shape[1]
    slots = kv_ref.shape[1]
    query_copy = pltpu.make_async_copy(
        arrived_ref.at[:, pl.ds(arrived_ref.shape[1] - query_count, query_count)], asked, sem
    )
    query_copy.start()
    top[...] = jnp.full(top.shape, NEG, jnp.float32)
    total[...] = jnp.zeros_like(total)
    mix[...] = jnp.zeros_like(mix)
    query_copy.wait()
    for slot in range(slots):
        owner = owner_ref[slot]
        keys = jnp.concatenate([kv_ref[0, slot, 0], kv_ref[1, slot, 0]], axis=0)
        found = lax.dot_general(asked[owner], keys, NT, preferred_element_type=jnp.float32) * score_scale
        score[slot] = found
        top[owner] = jnp.maximum(top[owner], found)
    for request in range(requests):
        top[request] = jnp.broadcast_to(jnp.max(top[request], axis=1, keepdims=True), top.shape[1:])
    for slot in range(slots):
        owner = owner_ref[slot]
        weights = jnp.exp(score[slot] - top[owner])
        values = jnp.concatenate([kv_ref[0, slot, 1], kv_ref[1, slot, 1]], axis=0)
        total[owner] = total[owner] + weights
        mix[owner] = mix[owner] + jnp.dot(
            weights.astype(jnp.bfloat16), values, preferred_element_type=jnp.float32
        )
    lane = lax.broadcasted_iota(jnp.int32, top.shape[1:], 1)
    for request in range(requests):
        norm = jnp.sum(total[request], axis=1, keepdims=True)
        held = norm > 0.0
        safe = jnp.where(held, norm, 1.0)
        out_ref[request, 0:query_count] = (mix[request] / safe).astype(jnp.bfloat16)
        level = jnp.where(held, top[request] + jnp.log(safe), NEG)
        high = level.astype(jnp.bfloat16).astype(jnp.float32)
        middle = (level - high).astype(jnp.bfloat16).astype(jnp.float32)
        low = level - high - middle
        terms = jnp.where(lane == 0, high, jnp.where(lane == 1, middle, jnp.where(lane == 2, low, 0.0)))
        out_ref[request, query_count : 2 * query_count] = terms.astype(jnp.bfloat16)


def resident(owner_of, arrived, pool_both, score_scale, query_count):
    requests, head_dim = arrived.shape[0], arrived.shape[2]
    slots = pool_both.shape[1]
    tokens = 2 * pool_both.shape[3]
    per_request = pltpu.VMEM((requests, query_count, head_dim), jnp.float32)
    return pl.pallas_call(
        functools.partial(resident_kernel, score_scale),
        out_shape=jax.ShapeDtypeStruct((requests, 2 * query_count, head_dim), jnp.bfloat16),
        in_specs=[
            pl.BlockSpec(memory_space=pltpu.SMEM),
            pl.BlockSpec(memory_space=pl.ANY),
            pl.BlockSpec(memory_space=pltpu.VMEM),
        ],
        out_specs=pl.BlockSpec(memory_space=pltpu.VMEM),
        scratch_shapes=[
            pltpu.VMEM((requests, query_count, head_dim), jnp.bfloat16),
            pltpu.VMEM((slots, query_count, tokens), jnp.float32),
            pltpu.VMEM((requests, query_count, tokens), jnp.float32),
            pltpu.VMEM((requests, query_count, tokens), jnp.float32),
            per_request,
            pltpu.SemaphoreType.DMA,
        ],
        compiler_params=pltpu.CompilerParams(vmem_limit_bytes=24 * 1024 * 1024),
        name="resident",
    )(owner_of, arrived, pool_both)


def finish_kernel(parts_ref, mix_ref, total_ref, top_ref, out_ref):
    query_count = mix_ref.shape[0]
    parts = parts_ref[...].astype(jnp.float32)
    outs, levels = parts[:, :query_count], parts[:, query_count:]
    levels = jnp.sum(levels, axis=2, keepdims=True)
    own_top = top_ref[...]
    joint = jnp.maximum(jnp.max(levels, axis=0), own_top)
    factor = jnp.exp(levels - joint[None])
    own_factor = jnp.exp(own_top - joint)
    norm = jnp.sum(factor, axis=0) + total_ref[...] * own_factor
    mixture = jnp.sum(outs * factor, axis=0) + mix_ref[...] * own_factor
    out_ref[...] = (mixture / norm).astype(jnp.bfloat16)


def finish(parts, own_mix, own_total, own_top):
    return pl.pallas_call(
        finish_kernel,
        out_shape=jax.ShapeDtypeStruct(own_mix.shape, jnp.bfloat16),
        in_specs=[pl.BlockSpec(memory_space=pltpu.VMEM)] * 4,
        out_specs=pl.BlockSpec(memory_space=pltpu.VMEM),
        name="finish",
    )(parts, own_mix, own_total, own_top)


def own_partial(query_rows, section_both, new_kv, length, pair_index, heads, score_scale):
    sectioned, half_len = section_both.shape[1], section_both.shape[3]
    steps = new_kv.shape[1]
    key_rows, value_rows = section_both[:, :, 0], section_both[:, :, 1]
    cached = (
        jnp.einsum("qd,bntd->qbnt", query_rows, key_rows, preferred_element_type=jnp.float32) * score_scale
    )
    page_count = (length + PAGE - 1) // PAGE
    page = page_count - sectioned + jnp.arange(sectioned, dtype=jnp.int32)
    position = (
        page[None, :, None] * PAGE
        + jnp.arange(2, dtype=jnp.int32)[:, None, None] * half_len
        + jnp.arange(half_len, dtype=jnp.int32)[None, None, :]
    )
    cached_mask = (position < length)[None]
    fresh = lax.dynamic_slice_in_dim(new_kv[0], pair_index, 1, 2)[:, :, 0]
    recent = (
        jnp.einsum("qd,jd->qj", query_rows, fresh[:, 0], preferred_element_type=jnp.float32) * score_scale
    )
    step = jnp.arange(query_rows.shape[0], dtype=jnp.int32) // heads
    recent_mask = jnp.arange(steps, dtype=jnp.int32)[None, :] <= step[:, None]
    cached = jnp.where(cached_mask, cached, NEG)
    recent = jnp.where(recent_mask, recent, NEG)
    top = jnp.maximum(jnp.max(cached, axis=(1, 2, 3)), jnp.max(recent, axis=1))[:, None]
    cached_weights = jnp.where(cached_mask, jnp.exp(cached - top[:, :, None, None]), 0.0)
    recent_weights = jnp.where(recent_mask, jnp.exp(recent - top), 0.0)
    total = jnp.sum(cached_weights, axis=(1, 2, 3)) + jnp.sum(recent_weights, axis=1)
    mix = jnp.einsum(
        "qbnt,bntd->qd", cached_weights.astype(jnp.bfloat16), value_rows, preferred_element_type=jnp.float32
    ) + jnp.einsum("qj,jd->qd", recent_weights.astype(jnp.bfloat16), fresh[:, 1], preferred_element_type=jnp.float32)
    return mix, jnp.broadcast_to(total[:, None], mix.shape), jnp.broadcast_to(top, mix.shape)


def shards(pool, sectioning, spill_to, tables, lengths, queries, new_kv):
    insts = lax.axis_size("inst")
    inst_index = lax.axis_index("inst")
    pair_index = lax.axis_index("pair")
    resident_slots, half_len, head_dim = pool.shape[0], pool.shape[3], pool.shape[4]
    sectioned = sectioning.shape[0]
    heads = queries.shape[2]
    query_count = queries.shape[1] * heads
    score_scale = head_dim ** (-0.5)
    query_rows = queries.reshape(query_count, head_dim)
    section_pages = sectioning.reshape(sectioned, 2 * half_len, head_dim)

    outgoing = pack(spill_to, section_pages, query_rows, insts)
    arrived = lax.all_to_all(outgoing, "inst", split_axis=0, concat_axis=0, tiled=True)

    pool_both = lax.all_gather(pool.reshape(pool.shape[0], 2, half_len, head_dim), "core", axis=0)
    section_both = lax.all_gather(sectioning.reshape(sectioned, 2, half_len, head_dim), "core", axis=0)
    held_here = (tables[:, :, 0] == inst_index)[:, :, None] & (
        tables[:, :, 1][:, :, None] == jnp.arange(resident_slots, dtype=jnp.int32)
    )
    request_ids = jnp.arange(tables.shape[0], dtype=jnp.int32)
    owner_of = jnp.sum(jnp.where(held_here, request_ids[:, None, None], 0), axis=(0, 1))
    length = lax.dynamic_index_in_dim(lengths, inst_index, 0, keepdims=False)
    own = own_partial(query_rows, section_both, new_kv, length, pair_index, heads, score_scale)

    partials = resident(owner_of, arrived, pool_both, score_scale, query_count)
    parts = lax.all_to_all(partials, "inst", split_axis=0, concat_axis=0, tiled=True)
    lent = arrived[:, : CAP * 2 * half_len].reshape(insts * CAP, 1, 2, half_len, head_dim)
    attended = finish(parts, *own)
    return attended.reshape(queries.shape), lent


def solution(mesh):
    insts, tp = mesh.devices.shape
    paired = Mesh(mesh.devices.reshape(insts, tp // 2, 2), ("inst", "pair", "core"))
    heads = ("pair", "core")
    return jax.shard_map(
        shards,
        mesh=paired,
        in_specs=(
            P("inst", heads),
            P("inst", heads),
            P("inst"),
            P(),
            P(),
            P("inst", None, heads),
            P("inst"),
        ),
        out_specs=(P("inst", None, heads), P("inst", heads)),
        check_vma=False,
    )
```

```python
import functools

import jax
import jax.numpy as jnp
from jax import lax
from jax.experimental import pallas as pl
from jax.experimental.pallas import tpu as pltpu
from jax.sharding import Mesh, PartitionSpec as P

PAGE = 128
CAP = 2
NEG = -1e30
NEW = 4
STAT_ROWS = 8
LENT_COPIES = 8
MIB = 1024 * 1024
NT = (((1,), (1,)), ((), ()))


def in_vmem(value):
    return pltpu.with_memory_space_constraint(value, pltpu.VMEM)


def in_hbm(value):
    return pltpu.with_memory_space_constraint(value, pltpu.HBM)


def plan_kernel(spill_ref, owner_ref, out_ref):
    sectioned, slots = spill_ref.shape[0], owner_ref.shape[0]
    insts = (out_ref.shape[0] - slots - sectioned) // (CAP + 1)
    empty, count = slots + sectioned, slots + sectioned + CAP * insts
    for slot in range(slots):
        out_ref[slot] = owner_ref[slot]
    for dest in range(insts):
        out_ref[count + dest] = 0
    for row in range(sectioned):
        dest = spill_ref[row]
        rank = out_ref[count + dest]
        out_ref[count + dest] = rank + 1
        out_ref[slots + row] = dest * CAP + rank
    found = jnp.int32(0)
    for dest in range(insts):
        filled = out_ref[count + dest]
        for rank in range(CAP):
            out_ref[empty + found] = dest * CAP + rank
            found = found + (filled <= rank).astype(jnp.int32)


def plan(spill_to, owner_of, insts):
    length = owner_of.shape[0] + spill_to.shape[0] + (CAP + 1) * insts
    return pl.pallas_call(
        plan_kernel,
        out_shape=pltpu.SMEM((length,), jnp.int32),
        in_specs=[pl.BlockSpec(memory_space=pltpu.SMEM)] * 2,
        out_specs=pl.BlockSpec(memory_space=pltpu.SMEM),
        compiler_params=pltpu.CompilerParams(vmem_limit_bytes=MIB),
        cost_estimate=pl.CostEstimate(flops=10**11, bytes_accessed=10**8, transcendentals=0),
        name="plan",
    )(in_hbm(spill_to), owner_of)


def resident_kernel(
    score_scale,
    plan_ref,
    asked_ref,
    near_ref,
    far_ref,
    section_ref,
    out_ref,
    pages,
    zeros,
    partials,
    score,
    top,
    total,
    mix,
    page_sem,
    slot_sem,
    part_sem,
):
    requests, query_count = mix.shape[0], mix.shape[1]
    slots = near_ref.shape[0]
    sectioned, rows = section_ref.shape[0], section_ref.shape[1]
    page_copy = pltpu.make_async_copy(section_ref, pages, page_sem)
    page_copy.start()
    zeros[...] = jnp.zeros_like(zeros)
    top[...] = jnp.full(top.shape, NEG, jnp.float32)
    total[...] = jnp.zeros_like(total)
    mix[...] = jnp.zeros_like(mix)

    def slot_copy(source, place):
        start = pl.multiple_of(lax.rem(place, CAP) * rows, rows)
        return pltpu.make_async_copy(source, out_ref.at[lax.div(place, CAP), pl.ds(start, rows)], slot_sem)

    for slot in range(slots):
        owner = plan_ref[slot]
        keys = jnp.concatenate([near_ref[slot, 0], far_ref[slot, 0]], axis=0)
        found = lax.dot_general(asked_ref[owner], keys, NT, preferred_element_type=jnp.float32) * score_scale
        score[slot] = found
        top[owner] = jnp.maximum(top[owner], found)

    page_copy.wait()

    @pl.loop(0, sectioned)
    def _(row):
        slot_copy(pages.at[row], plan_ref[slots + row]).start()

    @pl.loop(0, CAP * requests - sectioned)
    def _(row):
        slot_copy(zeros, plan_ref[slots + sectioned + row]).start()

    for request in range(requests):
        top[request] = jnp.broadcast_to(jnp.max(top[request], axis=1, keepdims=True), top.shape[1:])
    for slot in range(slots):
        owner = plan_ref[slot]
        weights = jnp.exp(score[slot] - top[owner])
        values = jnp.concatenate([near_ref[slot, 1], far_ref[slot, 1]], axis=0)
        total[owner] = total[owner] + weights
        mix[owner] = mix[owner] + jnp.dot(
            weights.astype(jnp.bfloat16), values, preferred_element_type=jnp.float32
        )
    gap = lax.broadcasted_iota(jnp.int32, top.shape[1:], 1) - lax.broadcasted_iota(jnp.int32, top.shape[1:], 0)
    stat_rows = partials.shape[1] - query_count
    for request in range(requests):
        norm = jnp.sum(total[request], axis=1, keepdims=True)
        held = norm > 0.0
        safe = jnp.where(held, norm, 1.0)
        partials[request, 0:query_count] = (mix[request] / safe).astype(jnp.bfloat16)
        level = jnp.where(held, top[request] + jnp.log(safe), NEG)
        high = level.astype(jnp.bfloat16).astype(jnp.float32)
        middle = (level - high).astype(jnp.bfloat16).astype(jnp.float32)
        low = level - high - middle
        terms = jnp.where(
            gap == 0, high, jnp.where(gap == query_count, middle, jnp.where(gap == 2 * query_count, low, 0.0))
        )
        terms = jnp.sum(terms, axis=0, keepdims=True)
        partials[request, query_count:] = jnp.broadcast_to(terms, (stat_rows, terms.shape[1])).astype(jnp.bfloat16)
    part_copy = pltpu.make_async_copy(partials, out_ref.at[:, pl.ds(CAP * rows, partials.shape[1])], part_sem)
    part_copy.start()
    part_copy.wait()
    all_slots = out_ref.at[:, pl.ds(0, CAP * rows)]
    pltpu.make_async_copy(all_slots, all_slots, slot_sem).wait()


def resident(steps_plan, asked, near, far, section_pages, score_scale):
    requests, query_count, head_dim = asked.shape
    slots = near.shape[0]
    tokens = 2 * near.shape[2]
    rows = section_pages.shape[1]
    part_rows = query_count + STAT_ROWS
    return pl.pallas_call(
        functools.partial(resident_kernel, score_scale),
        out_shape=pltpu.HBM((requests, CAP * rows + part_rows, head_dim), asked.dtype),
        in_specs=[
            pl.BlockSpec(memory_space=pltpu.SMEM),
            pl.BlockSpec(memory_space=pltpu.VMEM),
            pl.BlockSpec(memory_space=pltpu.VMEM),
            pl.BlockSpec(memory_space=pltpu.VMEM),
            pl.BlockSpec(memory_space=pl.ANY),
        ],
        out_specs=pl.BlockSpec(memory_space=pl.ANY),
        scratch_shapes=[
            pltpu.VMEM(section_pages.shape, section_pages.dtype),
            pltpu.VMEM(section_pages.shape[1:], section_pages.dtype),
            pltpu.VMEM((requests, part_rows, head_dim), asked.dtype),
            pltpu.VMEM((slots, query_count, tokens), jnp.float32),
            pltpu.VMEM((requests, query_count, tokens), jnp.float32),
            pltpu.VMEM((requests, query_count, tokens), jnp.float32),
            pltpu.VMEM((requests, query_count, head_dim), jnp.float32),
            pltpu.SemaphoreType.DMA,
            pltpu.SemaphoreType.DMA,
            pltpu.SemaphoreType.DMA,
        ],
        compiler_params=pltpu.CompilerParams(vmem_limit_bytes=16 * MIB),
        name="resident",
    )(steps_plan, in_vmem(asked), in_vmem(near), in_vmem(far), in_hbm(section_pages))


def own_kernel(score_scale, place_ref, query_ref, near_ref, far_ref, fresh_ref, out_ref):
    length, near_half = place_ref[0], place_ref[1]
    query_rows = query_ref[...]
    query_count, head_dim = query_rows.shape
    sectioned, half_len = near_ref.shape[0], near_ref.shape[2]
    first_page = (length + PAGE - 1) // PAGE - sectioned
    column = lax.broadcasted_iota(jnp.int32, (query_count, sectioned * half_len), 1)
    base = first_page * PAGE + column // half_len * PAGE + column % half_len
    scores, masks = [], []
    for half_ref, half in ((near_ref, near_half), (far_ref, 1 - near_half)):
        keys = half_ref[:, 0].reshape(sectioned * half_len, head_dim)
        found = lax.dot_general(query_rows, keys, NT, preferred_element_type=jnp.float32) * score_scale
        masks.append(base + half * half_len < length)
        scores.append(found)
    found = lax.dot_general(query_rows, fresh_ref[0], NT, preferred_element_type=jnp.float32) * score_scale
    step = lax.broadcasted_iota(jnp.int32, found.shape, 0) // (query_count // NEW)
    token = lax.broadcasted_iota(jnp.int32, found.shape, 1)
    masks.append(token <= step)
    scores.append(found)
    scores = [jnp.where(mask, found, NEG) for mask, found in zip(masks, scores, strict=True)]
    top = functools.reduce(jnp.maximum, [jnp.max(found, axis=1, keepdims=True) for found in scores])
    weights = [jnp.where(mask, jnp.exp(found - top), 0.0) for mask, found in zip(masks, scores, strict=True)]
    total = sum(jnp.sum(weight, axis=1, keepdims=True) for weight in weights)
    values = [
        near_ref[:, 1].reshape(sectioned * half_len, head_dim),
        far_ref[:, 1].reshape(sectioned * half_len, head_dim),
        fresh_ref[1],
    ]
    out_ref[0] = sum(
        jnp.dot(weight.astype(jnp.bfloat16), value, preferred_element_type=jnp.float32)
        for weight, value in zip(weights, values, strict=True)
    )
    out_ref[1] = jnp.broadcast_to(total, (query_count, head_dim))
    out_ref[2] = jnp.broadcast_to(top, (query_count, head_dim))


def own_partial(place, query_rows, near, far, fresh, score_scale):
    return pl.pallas_call(
        functools.partial(own_kernel, score_scale),
        out_shape=jax.ShapeDtypeStruct((3,) + query_rows.shape, jnp.float32),
        in_specs=[pl.BlockSpec(memory_space=pltpu.SMEM)] + [pl.BlockSpec(memory_space=pltpu.VMEM)] * 4,
        out_specs=pl.BlockSpec(memory_space=pltpu.VMEM),
        compiler_params=pltpu.CompilerParams(vmem_limit_bytes=16 * MIB),
        name="own_pages",
    )(place, query_rows, near, far, fresh)


def finish_kernel(arrived_ref, own_ref, out_ref, lent_ref, own, lent_sems, own_sem):
    insts, page_rows = lent_ref.shape[0], lent_ref.shape[1]
    query_count, head_dim = out_ref.shape
    pieces = lent_sems.shape[0]
    own_copy = pltpu.make_async_copy(own_ref, own, own_sem)
    own_copy.start()
    lent_copies = []
    for piece in range(pieces):
        part = pl.ds(piece * (insts // pieces), insts // pieces)
        lent_copies.append(
            pltpu.make_async_copy(
                arrived_ref.at[part, pl.ds(0, page_rows)], lent_ref.at[part], lent_sems.at[piece]
            )
        )
        lent_copies[-1].start()
    outs = arrived_ref[:, page_rows : page_rows + query_count].astype(jnp.float32)
    terms = arrived_ref[:, page_rows + query_count :].astype(jnp.float32)[:, 0:1]
    shape = (query_count, head_dim)
    lane = lax.broadcasted_iota(jnp.int32, shape, 1)
    own_lane = (lane % query_count == lax.broadcasted_iota(jnp.int32, shape, 0)) & (lane < 3 * query_count)
    levels = jnp.sum(jnp.where(own_lane[None], terms, 0.0), axis=2, keepdims=True)
    own_copy.wait()
    own_mix, own_total, own_top = own[0], own[1], own[2]
    joint = jnp.maximum(jnp.max(levels, axis=0), own_top)
    factor = jnp.exp(levels - joint[None])
    own_factor = jnp.exp(own_top - joint)
    norm = jnp.sum(factor, axis=0) + own_total * own_factor
    mixture = jnp.sum(outs * factor, axis=0) + own_mix * own_factor
    out_ref[...] = (mixture / norm).astype(jnp.bfloat16)
    for copy in lent_copies:
        copy.wait()


def finish(arrived, own, page_rows):
    insts, head_dim = arrived.shape[0], arrived.shape[2]
    return pl.pallas_call(
        finish_kernel,
        out_shape=(
            jax.ShapeDtypeStruct(own.shape[1:], jnp.bfloat16),
            pltpu.HBM((insts, page_rows, head_dim), arrived.dtype),
        ),
        in_specs=[pl.BlockSpec(memory_space=pltpu.VMEM), pl.BlockSpec(memory_space=pl.ANY)],
        out_specs=(pl.BlockSpec(memory_space=pltpu.VMEM), pl.BlockSpec(memory_space=pl.ANY)),
        scratch_shapes=[
            pltpu.VMEM(own.shape, own.dtype),
            pltpu.SemaphoreType.DMA((LENT_COPIES,)),
            pltpu.SemaphoreType.DMA,
        ],
        compiler_params=pltpu.CompilerParams(vmem_limit_bytes=8 * MIB),
        name="finish",
    )(in_vmem(arrived), in_hbm(own))


def shards(pool, sectioning, spill_to, tables, lengths, queries, new_kv):
    insts = lax.axis_size("inst")
    inst_index = lax.axis_index("inst")
    pair_index = lax.axis_index("pair")
    core = lax.axis_index("core")
    resident_slots, half_len, head_dim = pool.shape[0], pool.shape[3], pool.shape[4]
    sectioned = sectioning.shape[0]
    steps = queries.shape[1]
    query_count = steps * queries.shape[2]
    score_scale = head_dim ** (-0.5)
    query_rows = queries.reshape(query_count, head_dim)

    spread = jnp.broadcast_to(query_rows[None], (insts,) + query_rows.shape)
    asked = lax.all_to_all(spread, "inst", split_axis=0, concat_axis=0, tiled=True)

    section_pages = sectioning.reshape(sectioned, 2 * half_len, head_dim)
    near_pool = pool.reshape(resident_slots, 2, half_len, head_dim)
    near_section = sectioning.reshape(sectioned, 2, half_len, head_dim)
    far_pool = lax.ppermute(near_pool, "core", [(0, 1), (1, 0)])
    far_section = lax.ppermute(near_section, "core", [(0, 1), (1, 0)])
    held_here = (tables[:, :, 0] == inst_index)[:, :, None] & (
        tables[:, :, 1][:, :, None] == jnp.arange(resident_slots, dtype=jnp.int32)
    )
    request_ids = jnp.arange(tables.shape[0], dtype=jnp.int32)
    owner_of = jnp.sum(jnp.where(held_here, request_ids[:, None, None], 0), axis=(0, 1))
    length = lax.dynamic_index_in_dim(lengths, inst_index, 0, keepdims=False)
    place = jnp.stack([length, core.astype(jnp.int32)])
    fresh = lax.dynamic_slice_in_dim(new_kv[0], pair_index, 1, 2)[:, :, 0]
    fresh = jnp.pad(jnp.swapaxes(fresh, 0, 1), ((0, 0), (0, query_count - steps), (0, 0)))
    own = own_partial(place, query_rows, near_section, far_section, fresh, score_scale)

    steps_plan = plan(spill_to, owner_of, insts)
    outgoing = resident(steps_plan, asked, near_pool, far_pool, section_pages, score_scale)
    arrived = lax.all_to_all(outgoing, "inst", split_axis=0, concat_axis=0, tiled=True)
    attended, lent = finish(arrived, own, CAP * 2 * half_len)
    return attended.reshape(queries.shape), lent.reshape(insts * CAP, 1, 2, half_len, head_dim)


def solution(mesh):
    insts, tp = mesh.devices.shape
    paired = Mesh(mesh.devices.reshape(insts, tp // 2, 2), ("inst", "pair", "core"))
    heads = ("pair", "core")
    return jax.shard_map(
        shards,
        mesh=paired,
        in_specs=(
            P("inst", heads),
            P("inst", heads),
            P("inst"),
            P(),
            P(),
            P("inst", None, heads),
            P("inst"),
        ),
        out_specs=(P("inst", None, heads), P("inst", heads)),
        check_vma=False,
    )
```

```python
import functools

import jax
import jax.numpy as jnp
from jax import lax
from jax.experimental import pallas as pl
from jax.experimental.pallas import tpu as pltpu
from jax.sharding import Mesh, PartitionSpec as P

PAGE = 128
CAP = 2
NEG = -1e30
NEW = 4
STAT_ROWS = 8
MIB = 1024 * 1024
NT = (((1,), (1,)), ((), ()))


def in_vmem(value):
    return pltpu.with_memory_space_constraint(value, pltpu.VMEM)


def in_hbm(value):
    return pltpu.with_memory_space_constraint(value, pltpu.HBM)


def pack_kernel(
    spill_ref,
    section_ref,
    query_ref,
    whole_ref,
    paged_ref,
    asking_ref,
    spill,
    place,
    count,
    pages,
    zeros,
    asked,
    spread,
    sems,
):
    insts = whole_ref.shape[0]
    sectioned, rows = section_ref.shape[0], section_ref.shape[1]
    core = lax.axis_index("core")
    spill_copy = pltpu.make_async_copy(spill_ref, spill, sems.at[0])
    page_copy = pltpu.make_async_copy(section_ref, pages, sems.at[1])
    query_copy = pltpu.make_async_copy(query_ref, asked, sems.at[2])
    spill_copy.start()
    query_copy.start()
    page_copy.start()
    zeros[...] = jnp.zeros_like(zeros)
    for dest in range(insts):
        count[dest] = 0
    spill_copy.wait()

    @pl.loop(0, sectioned)
    def _(row):
        dest = spill[row]
        place[row] = count[dest]
        count[dest] = count[dest] + 1

    def lay_out(out_ref, query_rows_ref):
        def slot_copy(source, dest, rank):
            start = pl.multiple_of(rank * rows, rows)
            return pltpu.make_async_copy(source, out_ref.at[dest, pl.ds(start, rows)], sems.at[3])

        @pl.loop(0, insts)
        def _(dest):
            filled = count[dest]
            for rank in range(CAP):

                @pl.when(filled <= rank)
                def _():
                    slot_copy(zeros, dest, rank).start()

        query_copy.wait()
        spread[...] = jnp.broadcast_to(asked[...][None], spread.shape)
        spread_copy = pltpu.make_async_copy(spread, query_rows_ref, sems.at[4])
        spread_copy.start()
        page_copy.wait()

        @pl.loop(0, sectioned)
        def _(row):
            slot_copy(pages.at[row], spill[row], place[row]).start()

        all_slots = out_ref.at[:, pl.ds(0, CAP * rows)]
        pltpu.make_async_copy(all_slots, all_slots, sems.at[3]).wait()
        spread_copy.wait()

    @pl.when(core == 1)
    def _():
        lay_out(whole_ref, whole_ref.at[:, pl.ds(CAP * rows, asked.shape[0])])

    @pl.when(core == 0)
    def _():
        lay_out(paged_ref, asking_ref)


def pack(spill_to, section_pages, query_rows, insts):
    sectioned, rows, head_dim = section_pages.shape
    dtype = section_pages.dtype
    query_count = query_rows.shape[0]
    return pl.pallas_call(
        pack_kernel,
        out_shape=(
            pltpu.HBM((insts, CAP * rows + query_count, head_dim), dtype),
            pltpu.HBM((insts, CAP * rows + query_count + STAT_ROWS, head_dim), dtype),
            pltpu.HBM((insts, query_count, head_dim), dtype),
        ),
        in_specs=[pl.BlockSpec(memory_space=pl.ANY)] * 3,
        out_specs=[pl.BlockSpec(memory_space=pl.ANY)] * 3,
        scratch_shapes=[
            pltpu.SMEM(spill_to.shape, jnp.int32),
            pltpu.SMEM(spill_to.shape, jnp.int32),
            pltpu.SMEM((insts,), jnp.int32),
            pltpu.VMEM(section_pages.shape, dtype),
            pltpu.VMEM((rows, head_dim), dtype),
            pltpu.VMEM(query_rows.shape, dtype),
            pltpu.VMEM((insts,) + query_rows.shape, dtype),
            pltpu.SemaphoreType.DMA((5,)),
        ],
        compiler_params=pltpu.CompilerParams(vmem_limit_bytes=4 * MIB),
        name="pack",
    )(in_hbm(spill_to), in_hbm(section_pages), in_hbm(query_rows))


def resident_kernel(score_scale, staged, owner_ref, arrived_ref, near_ref, far_ref, *others):
    copies = []
    if staged:
        *others, near, far, sems = others
        for index in range(2):
            for source, target in ((near_ref, near), (far_ref, far)):
                copies.append(
                    pltpu.make_async_copy(source.at[:, index], target.at[:, index], sems.at[len(copies)])
                )
                copies[-1].start()
        near_ref, far_ref = near, far
    out_ref, partials, score, top, total, mix, part_sem = others[-7:]
    requests, query_count = mix.shape[0], mix.shape[1]
    slots = near_ref.shape[0]
    first_query = arrived_ref.shape[1] - query_count
    top[...] = jnp.full(top.shape, NEG, jnp.float32)
    total[...] = jnp.zeros_like(total)
    mix[...] = jnp.zeros_like(mix)

    for copy in copies[:2]:
        copy.wait()
    for slot in range(slots):
        owner = owner_ref[slot]
        keys = jnp.concatenate([near_ref[slot, 0], far_ref[slot, 0]], axis=0)
        found = lax.dot_general(arrived_ref[owner, first_query:], keys, NT, preferred_element_type=jnp.float32) * score_scale
        score[slot] = found
        top[owner] = jnp.maximum(top[owner], found)

    for request in range(requests):
        top[request] = jnp.broadcast_to(jnp.max(top[request], axis=1, keepdims=True), top.shape[1:])
    for copy in copies[2:]:
        copy.wait()
    for slot in range(slots):
        owner = owner_ref[slot]
        weights = jnp.exp(score[slot] - top[owner])
        values = jnp.concatenate([near_ref[slot, 1], far_ref[slot, 1]], axis=0)
        total[owner] = total[owner] + weights
        mix[owner] = mix[owner] + jnp.dot(
            weights.astype(jnp.bfloat16), values, preferred_element_type=jnp.float32
        )
    gap = lax.broadcasted_iota(jnp.int32, top.shape[1:], 1) - lax.broadcasted_iota(jnp.int32, top.shape[1:], 0)
    stat_rows = partials.shape[1] - query_count
    for request in range(requests):
        norm = jnp.sum(total[request], axis=1, keepdims=True)
        held = norm > 0.0
        safe = jnp.where(held, norm, 1.0)
        partials[request, 0:query_count] = (mix[request] / safe).astype(jnp.bfloat16)
        level = jnp.where(held, top[request] + jnp.log(safe), NEG)
        high = level.astype(jnp.bfloat16).astype(jnp.float32)
        middle = (level - high).astype(jnp.bfloat16).astype(jnp.float32)
        low = level - high - middle
        terms = jnp.where(
            gap == 0, high, jnp.where(gap == query_count, middle, jnp.where(gap == 2 * query_count, low, 0.0))
        )
        terms = jnp.sum(terms, axis=0, keepdims=True)
        partials[request, query_count:] = jnp.broadcast_to(terms, (stat_rows, terms.shape[1])).astype(jnp.bfloat16)
    part_rows = partials.shape[1]
    part_copy = pltpu.make_async_copy(
        partials, out_ref.at[:, pl.ds(out_ref.shape[1] - part_rows, part_rows)], part_sem
    )
    part_copy.start()
    part_copy.wait()


def resident(owner_of, arrived, near, far, outgoing, score_scale, query_count):
    requests, head_dim = arrived.shape[0], arrived.shape[2]
    slots, tokens = near.shape[0], 2 * near.shape[2]
    part_rows = query_count + STAT_ROWS
    out_shape, aliases = (requests, part_rows, head_dim), {}
    staged = outgoing is None
    operands = [owner_of, in_vmem(arrived)]
    spaces = [pltpu.SMEM, pltpu.VMEM]
    scratch = [
        pltpu.VMEM((requests, part_rows, head_dim), arrived.dtype),
        pltpu.VMEM((slots, query_count, tokens), jnp.float32),
        pltpu.VMEM((requests, query_count, tokens), jnp.float32),
        pltpu.VMEM((requests, query_count, tokens), jnp.float32),
        pltpu.VMEM((requests, query_count, head_dim), jnp.float32),
        pltpu.SemaphoreType.DMA,
    ]
    if staged:
        operands += [near, far]
        spaces += [pl.ANY] * 2
        scratch += [pltpu.VMEM(near.shape, near.dtype)] * 2 + [pltpu.SemaphoreType.DMA((4,))]
    else:
        out_shape, aliases = outgoing.shape, {4: 0}
        operands += [in_vmem(near), in_vmem(far), in_hbm(outgoing)]
        spaces += [pltpu.VMEM] * 2 + [pl.ANY]
    return pl.pallas_call(
        functools.partial(resident_kernel, score_scale, staged),
        out_shape=pltpu.HBM(out_shape, arrived.dtype),
        in_specs=[pl.BlockSpec(memory_space=space) for space in spaces],
        out_specs=pl.BlockSpec(memory_space=pl.ANY),
        scratch_shapes=scratch,
        input_output_aliases=aliases,
        compiler_params=pltpu.CompilerParams(vmem_limit_bytes=8 * MIB),
        name="resident_staged" if staged else "resident",
    )(*operands)


def own_kernel(score_scale, place_ref, query_ref, near_ref, far_ref, fresh_ref, out_ref):
    length, near_half = place_ref[0], place_ref[1]
    query_rows = query_ref[...]
    query_count, head_dim = query_rows.shape
    sectioned, half_len = near_ref.shape[0], near_ref.shape[2]
    first_page = (length + PAGE - 1) // PAGE - sectioned
    column = lax.broadcasted_iota(jnp.int32, (query_count, sectioned * half_len), 1)
    base = first_page * PAGE + column // half_len * PAGE + column % half_len
    scores, masks = [], []
    for half_ref, half in ((near_ref, near_half), (far_ref, 1 - near_half)):
        keys = half_ref[:, 0].reshape(sectioned * half_len, head_dim)
        found = lax.dot_general(query_rows, keys, NT, preferred_element_type=jnp.float32) * score_scale
        masks.append(base + half * half_len < length)
        scores.append(found)
    found = lax.dot_general(query_rows, fresh_ref[0], NT, preferred_element_type=jnp.float32) * score_scale
    step = lax.broadcasted_iota(jnp.int32, found.shape, 0) // (query_count // NEW)
    token = lax.broadcasted_iota(jnp.int32, found.shape, 1)
    masks.append(token <= step)
    scores.append(found)
    scores = [jnp.where(mask, found, NEG) for mask, found in zip(masks, scores, strict=True)]
    top = functools.reduce(jnp.maximum, [jnp.max(found, axis=1, keepdims=True) for found in scores])
    weights = [jnp.where(mask, jnp.exp(found - top), 0.0) for mask, found in zip(masks, scores, strict=True)]
    total = sum(jnp.sum(weight, axis=1, keepdims=True) for weight in weights)
    values = [
        near_ref[:, 1].reshape(sectioned * half_len, head_dim),
        far_ref[:, 1].reshape(sectioned * half_len, head_dim),
        fresh_ref[1],
    ]
    out_ref[0] = sum(
        jnp.dot(weight.astype(jnp.bfloat16), value, preferred_element_type=jnp.float32)
        for weight, value in zip(weights, values, strict=True)
    )
    out_ref[1] = jnp.broadcast_to(total, (query_count, head_dim))
    out_ref[2] = jnp.broadcast_to(top, (query_count, head_dim))


def own_partial(place, query_rows, near, far, fresh, score_scale):
    return pl.pallas_call(
        functools.partial(own_kernel, score_scale),
        out_shape=jax.ShapeDtypeStruct((3,) + query_rows.shape, jnp.float32),
        in_specs=[pl.BlockSpec(memory_space=pltpu.SMEM)] + [pl.BlockSpec(memory_space=pltpu.VMEM)] * 4,
        out_specs=pl.BlockSpec(memory_space=pltpu.VMEM),
        compiler_params=pltpu.CompilerParams(vmem_limit_bytes=16 * MIB),
        name="own_pages",
    )(place, query_rows, near, far, fresh)


def lend_kernel(arrived_ref, lent_ref, sem):
    lent_copy = pltpu.make_async_copy(arrived_ref.at[:, pl.ds(0, lent_ref.shape[1])], lent_ref, sem)
    lent_copy.start()
    lent_copy.wait()


def lend(arrived, page_rows):
    insts, head_dim = arrived.shape[0], arrived.shape[2]
    return pl.pallas_call(
        lend_kernel,
        out_shape=pltpu.HBM((insts, page_rows, head_dim), arrived.dtype),
        in_specs=[pl.BlockSpec(memory_space=pl.ANY)],
        out_specs=pl.BlockSpec(memory_space=pl.ANY),
        scratch_shapes=[pltpu.SemaphoreType.DMA],
        compiler_params=pltpu.CompilerParams(vmem_limit_bytes=MIB),
        name="lend",
    )(in_vmem(arrived))


def join(arrived_ref, own_ref, out_ref, own, own_sem):
    query_count, head_dim = out_ref.shape
    first_row = arrived_ref.shape[1] - query_count - STAT_ROWS
    own_copy = pltpu.make_async_copy(own_ref, own, own_sem)
    own_copy.start()
    outs = arrived_ref[:, first_row : first_row + query_count].astype(jnp.float32)
    terms = arrived_ref[:, first_row + query_count :].astype(jnp.float32)[:, 0:1]
    shape = (query_count, head_dim)
    lane = lax.broadcasted_iota(jnp.int32, shape, 1)
    own_lane = (lane % query_count == lax.broadcasted_iota(jnp.int32, shape, 0)) & (lane < 3 * query_count)
    levels = jnp.sum(jnp.where(own_lane[None], terms, 0.0), axis=2, keepdims=True)
    own_copy.wait()
    own_mix, own_total, own_top = own[0], own[1], own[2]
    joint = jnp.maximum(jnp.max(levels, axis=0), own_top)
    factor = jnp.exp(levels - joint[None])
    own_factor = jnp.exp(own_top - joint)
    norm = jnp.sum(factor, axis=0) + own_total * own_factor
    mixture = jnp.sum(outs * factor, axis=0) + own_mix * own_factor
    out_ref[...] = (mixture / norm).astype(jnp.bfloat16)


def finish_kernel(arrived_ref, own_ref, out_ref, lent_ref, own, own_sem, lent_sem):
    lent_copy = pltpu.make_async_copy(arrived_ref.at[:, pl.ds(0, lent_ref.shape[1])], lent_ref, lent_sem)
    lent_copy.start()
    join(arrived_ref, own_ref, out_ref, own, own_sem)
    lent_copy.wait()


def finish(arrived, own, page_rows):
    insts, head_dim = arrived.shape[0], arrived.shape[2]
    attended = jax.ShapeDtypeStruct(own.shape[1:], jnp.bfloat16)
    scratch = [pltpu.VMEM(own.shape, own.dtype), pltpu.SemaphoreType.DMA]
    in_place = pl.BlockSpec(memory_space=pl.ANY)
    if page_rows:
        attended = (attended, pltpu.HBM((insts, page_rows, head_dim), arrived.dtype))
        scratch.append(pltpu.SemaphoreType.DMA)
    return pl.pallas_call(
        finish_kernel if page_rows else join,
        out_shape=attended,
        in_specs=[pl.BlockSpec(memory_space=pltpu.VMEM), in_place],
        out_specs=(pl.BlockSpec(memory_space=pltpu.VMEM), in_place)
        if page_rows
        else pl.BlockSpec(memory_space=pltpu.VMEM),
        scratch_shapes=scratch,
        compiler_params=pltpu.CompilerParams(vmem_limit_bytes=8 * MIB),
        name="finish" if page_rows else "join",
    )(in_vmem(arrived), in_hbm(own))


def shards(pool, sectioning, spill_to, tables, lengths, queries, new_kv):
    insts = lax.axis_size("inst")
    resident_slots, half_len, head_dim = pool.shape[0], pool.shape[3], pool.shape[4]
    sectioned = sectioning.shape[0]
    steps = queries.shape[1]
    query_count = steps * queries.shape[2]
    score_scale = head_dim ** (-0.5)
    query_rows = queries.reshape(query_count, head_dim)

    section_pages = sectioning.reshape(sectioned, 2 * half_len, head_dim)
    page_rows = CAP * 2 * half_len
    near_pool = pool.reshape(resident_slots, 2, half_len, head_dim)
    near_section = sectioning.reshape(sectioned, 2, half_len, head_dim)
    far_pool = lax.ppermute(near_pool, "core", [(0, 1), (1, 0)])
    far_section = lax.ppermute(near_section, "core", [(0, 1), (1, 0)])
    whole, paged, asking = pack(spill_to, section_pages, query_rows, insts)

    def exchange(outgoing):
        return lax.all_to_all(outgoing, "inst", split_axis=0, concat_axis=0, tiled=True)

    def owners():
        held_here = (tables[:, :, 0] == lax.axis_index("inst"))[:, :, None] & (
            tables[:, :, 1][:, :, None] == jnp.arange(resident_slots, dtype=jnp.int32)
        )
        request_ids = jnp.arange(tables.shape[0], dtype=jnp.int32)
        return jnp.sum(jnp.where(held_here, request_ids[:, None, None], 0), axis=(0, 1))

    def own_part(far_section):
        length = lax.dynamic_index_in_dim(lengths, lax.axis_index("inst"), 0, keepdims=False)
        place = jnp.stack([length, lax.axis_index("core").astype(jnp.int32)])
        fresh = lax.dynamic_slice_in_dim(new_kv[0], lax.axis_index("pair"), 1, 2)[:, :, 0]
        fresh = jnp.pad(jnp.swapaxes(fresh, 0, 1), ((0, 0), (0, query_count - steps), (0, 0)))
        return own_partial(place, query_rows, near_section, far_section, fresh, score_scale)

    def queries_first(whole, paged, asking, far_pool, far_section):
        asked = exchange(asking)
        own = own_part(far_section)
        paged = resident(owners(), asked, near_pool, far_pool, paged, score_scale, query_count)
        return finish(exchange(paged), own, page_rows)

    def pages_first(whole, paged, asking, far_pool, far_section):
        arrived = exchange(whole)
        own = own_part(far_section)
        partials = resident(owners(), arrived, near_pool, far_pool, None, score_scale, query_count)
        lent = lend(arrived, page_rows)
        return finish(exchange(partials), own, 0), lent

    attended, lent = lax.cond(
        lax.axis_index("core") == 0, queries_first, pages_first, whole, paged, asking, far_pool, far_section
    )
    return attended.reshape(queries.shape), lent.reshape(insts * CAP, 1, 2, half_len, head_dim)


def solution(mesh):
    insts, tp = mesh.devices.shape
    paired = Mesh(mesh.devices.reshape(insts, tp // 2, 2), ("inst", "pair", "core"))
    heads = ("pair", "core")
    return jax.shard_map(
        shards,
        mesh=paired,
        in_specs=(
            P("inst", heads),
            P("inst", heads),
            P("inst"),
            P(),
            P(),
            P("inst", None, heads),
            P("inst"),
        ),
        out_specs=(P("inst", None, heads), P("inst", heads)),
        check_vma=False,
    )
```

```python
import functools

import jax
import jax.numpy as jnp
from jax import lax
from jax.experimental import pallas as pl
from jax.experimental.pallas import tpu as pltpu
from jax.sharding import Mesh, PartitionSpec as P

PAGE = 128
CAP = 2
NEG = -1e30
NEW = 4
STAT_ROWS = 8
MIB = 1024 * 1024
NT = (((1,), (1,)), ((), ()))


def in_vmem(value):
    return pltpu.with_memory_space_constraint(value, pltpu.VMEM)


def in_hbm(value):
    return pltpu.with_memory_space_constraint(value, pltpu.HBM)


def pack_kernel(
    spill_ref,
    section_ref,
    query_ref,
    whole_ref,
    paged_ref,
    asking_ref,
    spill,
    place,
    count,
    pages,
    zeros,
    asked,
    spread,
    sems,
):
    insts = whole_ref.shape[0]
    sectioned, rows = section_ref.shape[0], section_ref.shape[1]
    core = lax.axis_index("core")
    spill_copy = pltpu.make_async_copy(spill_ref, spill, sems.at[0])
    page_copy = pltpu.make_async_copy(section_ref, pages, sems.at[1])
    query_copy = pltpu.make_async_copy(query_ref, asked, sems.at[2])
    spill_copy.start()
    query_copy.start()
    page_copy.start()
    zeros[...] = jnp.zeros_like(zeros)
    for dest in range(insts):
        count[dest] = 0
    spill_copy.wait()

    @pl.loop(0, sectioned)
    def _(row):
        dest = spill[row]
        place[row] = count[dest]
        count[dest] = count[dest] + 1

    def lay_out(out_ref, query_rows_ref):
        def slot_copy(source, dest, rank):
            start = pl.multiple_of(rank * rows, rows)
            return pltpu.make_async_copy(source, out_ref.at[dest, pl.ds(start, rows)], sems.at[3])

        @pl.loop(0, insts)
        def _(dest):
            filled = count[dest]
            for rank in range(CAP):

                @pl.when(filled <= rank)
                def _():
                    slot_copy(zeros, dest, rank).start()

        query_copy.wait()
        spread[...] = jnp.broadcast_to(asked[...][None], spread.shape)
        spread_copy = pltpu.make_async_copy(spread, query_rows_ref, sems.at[4])
        spread_copy.start()
        page_copy.wait()

        @pl.loop(0, sectioned)
        def _(row):
            slot_copy(pages.at[row], spill[row], place[row]).start()

        all_slots = out_ref.at[:, pl.ds(0, CAP * rows)]
        pltpu.make_async_copy(all_slots, all_slots, sems.at[3]).wait()
        spread_copy.wait()

    @pl.when(core == 1)
    def _():
        lay_out(whole_ref, whole_ref.at[:, pl.ds(CAP * rows, asked.shape[0])])

    @pl.when(core == 0)
    def _():
        lay_out(paged_ref, asking_ref)


def pack(spill_to, section_pages, query_rows, insts):
    sectioned, rows, head_dim = section_pages.shape
    dtype = section_pages.dtype
    query_count = query_rows.shape[0]
    return pl.pallas_call(
        pack_kernel,
        out_shape=(
            pltpu.HBM((insts, CAP * rows + query_count, head_dim), dtype),
            pltpu.HBM((insts, CAP * rows + query_count + STAT_ROWS, head_dim), dtype),
            pltpu.HBM((insts, query_count, head_dim), dtype),
        ),
        in_specs=[pl.BlockSpec(memory_space=pl.ANY)] * 3,
        out_specs=[pl.BlockSpec(memory_space=pl.ANY)] * 3,
        scratch_shapes=[
            pltpu.SMEM(spill_to.shape, jnp.int32),
            pltpu.SMEM(spill_to.shape, jnp.int32),
            pltpu.SMEM((insts,), jnp.int32),
            pltpu.VMEM(section_pages.shape, dtype),
            pltpu.VMEM((rows, head_dim), dtype),
            pltpu.VMEM(query_rows.shape, dtype),
            pltpu.VMEM((insts,) + query_rows.shape, dtype),
            pltpu.SemaphoreType.DMA((5,)),
        ],
        compiler_params=pltpu.CompilerParams(vmem_limit_bytes=4 * MIB),
        name="pack",
    )(in_hbm(spill_to), in_hbm(section_pages), in_hbm(query_rows))


def resident_kernel(score_scale, staged, owner_ref, arrived_ref, near_ref, far_ref, *others):
    if staged:
        *others, asked, near, sems = others
        query_count = asked.shape[1]
        first_query = arrived_ref.shape[1] - query_count
        copies = [
            pltpu.make_async_copy(arrived_ref.at[:, pl.ds(first_query, query_count)], asked, sems.at[0]),
            pltpu.make_async_copy(near_ref.at[:, 0], near.at[:, 0], sems.at[1]),
            pltpu.make_async_copy(near_ref.at[:, 1], near.at[:, 1], sems.at[2]),
        ]
        for copy in copies:
            copy.start()
        arrived_ref, near_ref = asked, near
    out_ref, partials, score, top, total, mix, part_sem = others[-7:]
    requests, query_count = mix.shape[0], mix.shape[1]
    slots = near_ref.shape[0]
    top[...] = jnp.full(top.shape, NEG, jnp.float32)
    total[...] = jnp.zeros_like(total)
    mix[...] = jnp.zeros_like(mix)

    if staged:
        copies[0].wait()
        copies[1].wait()
    for slot in range(slots):
        owner = owner_ref[slot]
        keys = jnp.concatenate([near_ref[slot, 0], far_ref[slot, 0]], axis=0)
        found = lax.dot_general(arrived_ref[owner], keys, NT, preferred_element_type=jnp.float32) * score_scale
        score[slot] = found
        top[owner] = jnp.maximum(top[owner], found)

    for request in range(requests):
        top[request] = jnp.broadcast_to(jnp.max(top[request], axis=1, keepdims=True), top.shape[1:])
    if staged:
        copies[2].wait()
    for slot in range(slots):
        owner = owner_ref[slot]
        weights = jnp.exp(score[slot] - top[owner])
        values = jnp.concatenate([near_ref[slot, 1], far_ref[slot, 1]], axis=0)
        total[owner] = total[owner] + weights
        mix[owner] = mix[owner] + jnp.dot(
            weights.astype(jnp.bfloat16), values, preferred_element_type=jnp.float32
        )
    gap = lax.broadcasted_iota(jnp.int32, top.shape[1:], 1) - lax.broadcasted_iota(jnp.int32, top.shape[1:], 0)
    stat_rows = partials.shape[1] - query_count
    for request in range(requests):
        norm = jnp.sum(total[request], axis=1, keepdims=True)
        held = norm > 0.0
        safe = jnp.where(held, norm, 1.0)
        partials[request, 0:query_count] = (mix[request] / safe).astype(jnp.bfloat16)
        level = jnp.where(held, top[request] + jnp.log(safe), NEG)
        high = level.astype(jnp.bfloat16).astype(jnp.float32)
        middle = (level - high).astype(jnp.bfloat16).astype(jnp.float32)
        low = level - high - middle
        terms = jnp.where(
            gap == 0, high, jnp.where(gap == query_count, middle, jnp.where(gap == 2 * query_count, low, 0.0))
        )
        terms = jnp.sum(terms, axis=0, keepdims=True)
        partials[request, query_count:] = jnp.broadcast_to(terms, (stat_rows, terms.shape[1])).astype(jnp.bfloat16)
    part_rows = partials.shape[1]
    part_copy = pltpu.make_async_copy(
        partials, out_ref.at[:, pl.ds(out_ref.shape[1] - part_rows, part_rows)], part_sem
    )
    part_copy.start()
    part_copy.wait()


def resident(owner_of, arrived, near, far, outgoing, score_scale, query_count):
    requests, head_dim = arrived.shape[0], arrived.shape[2]
    slots, tokens = near.shape[0], 2 * near.shape[2]
    part_rows = query_count + STAT_ROWS
    out_shape, aliases = (requests, part_rows, head_dim), {}
    staged = outgoing is None
    scratch = [
        pltpu.VMEM((requests, part_rows, head_dim), arrived.dtype),
        pltpu.VMEM((slots, query_count, tokens), jnp.float32),
        pltpu.VMEM((requests, query_count, tokens), jnp.float32),
        pltpu.VMEM((requests, query_count, tokens), jnp.float32),
        pltpu.VMEM((requests, query_count, head_dim), jnp.float32),
        pltpu.SemaphoreType.DMA,
    ]
    if staged:
        operands = [owner_of, arrived, in_hbm(near), in_vmem(far)]
        spaces = [pltpu.SMEM, pl.ANY, pl.ANY, pltpu.VMEM]
        scratch += [
            pltpu.VMEM((requests, query_count, head_dim), arrived.dtype),
            pltpu.VMEM(near.shape, near.dtype),
            pltpu.SemaphoreType.DMA((3,)),
        ]
    else:
        out_shape, aliases = outgoing.shape, {4: 0}
        operands = [owner_of, in_vmem(arrived), in_vmem(near), in_vmem(far), in_hbm(outgoing)]
        spaces = [pltpu.SMEM] + [pltpu.VMEM] * 3 + [pl.ANY]
    return pl.pallas_call(
        functools.partial(resident_kernel, score_scale, staged),
        out_shape=pltpu.HBM(out_shape, arrived.dtype),
        in_specs=[pl.BlockSpec(memory_space=space) for space in spaces],
        out_specs=pl.BlockSpec(memory_space=pl.ANY),
        scratch_shapes=scratch,
        input_output_aliases=aliases,
        compiler_params=pltpu.CompilerParams(vmem_limit_bytes=8 * MIB),
        name="resident_staged" if staged else "resident",
    )(*operands)


def own_kernel(score_scale, place_ref, query_ref, near_ref, far_ref, fresh_ref, out_ref):
    length, near_half = place_ref[0], place_ref[1]
    query_rows = query_ref[...]
    query_count, head_dim = query_rows.shape
    sectioned, half_len = near_ref.shape[0], near_ref.shape[2]
    first_page = (length + PAGE - 1) // PAGE - sectioned
    column = lax.broadcasted_iota(jnp.int32, (query_count, sectioned * half_len), 1)
    base = first_page * PAGE + column // half_len * PAGE + column % half_len
    scores, masks = [], []
    for half_ref, half in ((near_ref, near_half), (far_ref, 1 - near_half)):
        keys = half_ref[:, 0].reshape(sectioned * half_len, head_dim)
        found = lax.dot_general(query_rows, keys, NT, preferred_element_type=jnp.float32) * score_scale
        masks.append(base + half * half_len < length)
        scores.append(found)
    found = lax.dot_general(query_rows, fresh_ref[0], NT, preferred_element_type=jnp.float32) * score_scale
    step = lax.broadcasted_iota(jnp.int32, found.shape, 0) // (query_count // NEW)
    token = lax.broadcasted_iota(jnp.int32, found.shape, 1)
    masks.append(token <= step)
    scores.append(found)
    scores = [jnp.where(mask, found, NEG) for mask, found in zip(masks, scores, strict=True)]
    top = functools.reduce(jnp.maximum, [jnp.max(found, axis=1, keepdims=True) for found in scores])
    weights = [jnp.where(mask, jnp.exp(found - top), 0.0) for mask, found in zip(masks, scores, strict=True)]
    total = sum(jnp.sum(weight, axis=1, keepdims=True) for weight in weights)
    values = [
        near_ref[:, 1].reshape(sectioned * half_len, head_dim),
        far_ref[:, 1].reshape(sectioned * half_len, head_dim),
        fresh_ref[1],
    ]
    out_ref[0] = sum(
        jnp.dot(weight.astype(jnp.bfloat16), value, preferred_element_type=jnp.float32)
        for weight, value in zip(weights, values, strict=True)
    )
    out_ref[1] = jnp.broadcast_to(total, (query_count, head_dim))
    out_ref[2] = jnp.broadcast_to(top, (query_count, head_dim))


def own_partial(place, query_rows, near, far, fresh, score_scale):
    return pl.pallas_call(
        functools.partial(own_kernel, score_scale),
        out_shape=jax.ShapeDtypeStruct((3,) + query_rows.shape, jnp.float32),
        in_specs=[pl.BlockSpec(memory_space=pltpu.SMEM)] + [pl.BlockSpec(memory_space=pltpu.VMEM)] * 4,
        out_specs=pl.BlockSpec(memory_space=pltpu.VMEM),
        compiler_params=pltpu.CompilerParams(vmem_limit_bytes=16 * MIB),
        name="own_pages",
    )(place, query_rows, near, far, fresh)


def lend_kernel(arrived_ref, lent_ref, pages, sems):
    pieces = sems.shape[0] // 2
    count = lent_ref.shape[0] // pieces
    arriving, leaving = [], []
    for piece in range(pieces):
        part = pl.ds(piece * count, count)
        arriving.append(
            pltpu.make_async_copy(
                arrived_ref.at[part, pl.ds(0, lent_ref.shape[1])], pages.at[part], sems.at[2 * piece]
            )
        )
        leaving.append(pltpu.make_async_copy(pages.at[part], lent_ref.at[part], sems.at[2 * piece + 1]))
        arriving[-1].start()
    for into, out in zip(arriving, leaving, strict=True):
        into.wait()
        out.start()
    for out in leaving:
        out.wait()


def lend(arrived, page_rows):
    insts, head_dim = arrived.shape[0], arrived.shape[2]
    return pl.pallas_call(
        lend_kernel,
        out_shape=pltpu.HBM((insts, page_rows, head_dim), arrived.dtype),
        in_specs=[pl.BlockSpec(memory_space=pl.ANY)],
        out_specs=pl.BlockSpec(memory_space=pl.ANY),
        scratch_shapes=[
            pltpu.VMEM((insts, page_rows, head_dim), arrived.dtype),
            pltpu.SemaphoreType.DMA((8,)),
        ],
        compiler_params=pltpu.CompilerParams(vmem_limit_bytes=4 * MIB),
        name="lend",
    )(arrived)


def join(arrived_ref, own_ref, out_ref, own, own_sem):
    query_count, head_dim = out_ref.shape
    first_row = arrived_ref.shape[1] - query_count - STAT_ROWS
    own_copy = pltpu.make_async_copy(own_ref, own, own_sem)
    own_copy.start()
    outs = arrived_ref[:, first_row : first_row + query_count].astype(jnp.float32)
    terms = arrived_ref[:, first_row + query_count :].astype(jnp.float32)[:, 0:1]
    shape = (query_count, head_dim)
    lane = lax.broadcasted_iota(jnp.int32, shape, 1)
    own_lane = (lane % query_count == lax.broadcasted_iota(jnp.int32, shape, 0)) & (lane < 3 * query_count)
    levels = jnp.sum(jnp.where(own_lane[None], terms, 0.0), axis=2, keepdims=True)
    own_copy.wait()
    own_mix, own_total, own_top = own[0], own[1], own[2]
    joint = jnp.maximum(jnp.max(levels, axis=0), own_top)
    factor = jnp.exp(levels - joint[None])
    own_factor = jnp.exp(own_top - joint)
    norm = jnp.sum(factor, axis=0) + own_total * own_factor
    mixture = jnp.sum(outs * factor, axis=0) + own_mix * own_factor
    out_ref[...] = (mixture / norm).astype(jnp.bfloat16)


def finish_kernel(arrived_ref, own_ref, out_ref, lent_ref, own, own_sem, lent_sem):
    lent_copy = pltpu.make_async_copy(arrived_ref.at[:, pl.ds(0, lent_ref.shape[1])], lent_ref, lent_sem)
    lent_copy.start()
    join(arrived_ref, own_ref, out_ref, own, own_sem)
    lent_copy.wait()


def finish(arrived, own, page_rows):
    insts, head_dim = arrived.shape[0], arrived.shape[2]
    attended = jax.ShapeDtypeStruct(own.shape[1:], jnp.bfloat16)
    scratch = [pltpu.VMEM(own.shape, own.dtype), pltpu.SemaphoreType.DMA]
    in_place = pl.BlockSpec(memory_space=pl.ANY)
    if page_rows:
        attended = (attended, pltpu.HBM((insts, page_rows, head_dim), arrived.dtype))
        scratch.append(pltpu.SemaphoreType.DMA)
    return pl.pallas_call(
        finish_kernel if page_rows else join,
        out_shape=attended,
        in_specs=[pl.BlockSpec(memory_space=pltpu.VMEM), in_place],
        out_specs=(pl.BlockSpec(memory_space=pltpu.VMEM), in_place)
        if page_rows
        else pl.BlockSpec(memory_space=pltpu.VMEM),
        scratch_shapes=scratch,
        compiler_params=pltpu.CompilerParams(vmem_limit_bytes=8 * MIB),
        name="finish" if page_rows else "join",
    )(in_vmem(arrived), in_hbm(own))


def shards(pool, sectioning, spill_to, tables, lengths, queries, new_kv):
    insts = lax.axis_size("inst")
    resident_slots, half_len, head_dim = pool.shape[0], pool.shape[3], pool.shape[4]
    sectioned = sectioning.shape[0]
    steps = queries.shape[1]
    query_count = steps * queries.shape[2]
    score_scale = head_dim ** (-0.5)
    query_rows = queries.reshape(query_count, head_dim)

    section_pages = sectioning.reshape(sectioned, 2 * half_len, head_dim)
    page_rows = CAP * 2 * half_len
    near_pool = pool.reshape(resident_slots, 2, half_len, head_dim)
    near_section = sectioning.reshape(sectioned, 2, half_len, head_dim)
    far_pool = lax.ppermute(near_pool, "core", [(0, 1), (1, 0)])
    far_section = lax.ppermute(near_section, "core", [(0, 1), (1, 0)])
    whole, paged, asking = pack(spill_to, section_pages, query_rows, insts)

    def exchange(outgoing):
        return lax.all_to_all(outgoing, "inst", split_axis=0, concat_axis=0, tiled=True)

    def owners():
        held_here = (tables[:, :, 0] == lax.axis_index("inst"))[:, :, None] & (
            tables[:, :, 1][:, :, None] == jnp.arange(resident_slots, dtype=jnp.int32)
        )
        request_ids = jnp.arange(tables.shape[0], dtype=jnp.int32)
        return jnp.sum(jnp.where(held_here, request_ids[:, None, None], 0), axis=(0, 1))

    def own_part(far_section):
        length = lax.dynamic_index_in_dim(lengths, lax.axis_index("inst"), 0, keepdims=False)
        place = jnp.stack([length, lax.axis_index("core").astype(jnp.int32)])
        fresh = lax.dynamic_slice_in_dim(new_kv[0], lax.axis_index("pair"), 1, 2)[:, :, 0]
        fresh = jnp.pad(jnp.swapaxes(fresh, 0, 1), ((0, 0), (0, query_count - steps), (0, 0)))
        return own_partial(place, query_rows, near_section, far_section, fresh, score_scale)

    def queries_first(whole, paged, asking, far_pool, far_section):
        asked = exchange(asking)
        own = own_part(far_section)
        paged = resident(owners(), asked, near_pool, far_pool, paged, score_scale, query_count)
        return finish(exchange(paged), own, page_rows)

    def pages_first(whole, paged, asking, far_pool, far_section):
        arrived = exchange(whole)
        own = own_part(far_section)
        partials = resident(owners(), arrived, near_pool, far_pool, None, score_scale, query_count)
        lent = lend(arrived, page_rows)
        return finish(exchange(partials), own, 0), lent

    attended, lent = lax.cond(
        lax.axis_index("core") == 0, queries_first, pages_first, whole, paged, asking, far_pool, far_section
    )
    return attended.reshape(queries.shape), lent.reshape(insts * CAP, 1, 2, half_len, head_dim)


def solution(mesh):
    insts, tp = mesh.devices.shape
    paired = Mesh(mesh.devices.reshape(insts, tp // 2, 2), ("inst", "pair", "core"))
    heads = ("pair", "core")
    return jax.shard_map(
        shards,
        mesh=paired,
        in_specs=(
            P("inst", heads),
            P("inst", heads),
            P("inst"),
            P(),
            P(),
            P("inst", None, heads),
            P("inst"),
        ),
        out_specs=(P("inst", None, heads), P("inst", heads)),
        check_vma=False,
    )
```

```python
import functools

import jax
import jax.numpy as jnp
from jax import lax
from jax.experimental import pallas as pl
from jax.experimental.pallas import tpu as pltpu
from jax.sharding import Mesh, PartitionSpec as P

PAGE = 128
CAP = 2
NEG = -1e30
NEW = 4
STAT_ROWS = 16
MIB = 1024 * 1024
NT = (((1,), (1,)), ((), ()))


def in_vmem(value):
    return pltpu.with_memory_space_constraint(value, pltpu.VMEM)


def in_hbm(value):
    return pltpu.with_memory_space_constraint(value, pltpu.HBM)


def pack_kernel(
    spill_ref,
    section_ref,
    query_ref,
    whole_ref,
    paged_ref,
    asking_ref,
    spill,
    place,
    count,
    pages,
    zeros,
    asked,
    spread,
    sems,
):
    insts = whole_ref.shape[0]
    sectioned, rows = section_ref.shape[0], section_ref.shape[1]
    core = lax.axis_index("core")
    spill_copy = pltpu.make_async_copy(spill_ref, spill, sems.at[0])
    page_copy = pltpu.make_async_copy(section_ref, pages, sems.at[1])
    query_copy = pltpu.make_async_copy(query_ref, asked, sems.at[2])
    spill_copy.start()
    query_copy.start()
    page_copy.start()
    zeros[...] = jnp.zeros_like(zeros)
    for dest in range(insts):
        count[dest] = 0
    spill_copy.wait()

    @pl.loop(0, sectioned)
    def _(row):
        dest = spill[row]
        place[row] = count[dest]
        count[dest] = count[dest] + 1

    def lay_out(out_ref, query_rows_ref):
        def slot_copy(source, dest, rank):
            start = pl.multiple_of(rank * rows, rows)
            return pltpu.make_async_copy(source, out_ref.at[dest, pl.ds(start, rows)], sems.at[3])

        @pl.loop(0, insts)
        def _(dest):
            filled = count[dest]
            for rank in range(CAP):

                @pl.when(filled <= rank)
                def _():
                    slot_copy(zeros, dest, rank).start()

        query_copy.wait()
        spread[...] = jnp.broadcast_to(asked[...][None], spread.shape)
        spread_copy = pltpu.make_async_copy(spread, query_rows_ref, sems.at[4])
        spread_copy.start()
        page_copy.wait()

        @pl.loop(0, sectioned)
        def _(row):
            slot_copy(pages.at[row], spill[row], place[row]).start()

        all_slots = out_ref.at[:, pl.ds(0, CAP * rows)]
        pltpu.make_async_copy(all_slots, all_slots, sems.at[3]).wait()
        spread_copy.wait()

    @pl.when(core == 1)
    def _():
        lay_out(whole_ref, whole_ref.at[:, pl.ds(CAP * rows, asked.shape[0])])

    @pl.when(core == 0)
    def _():
        lay_out(paged_ref, asking_ref)


def pack(spill_to, section_pages, query_rows, insts):
    sectioned, rows, head_dim = section_pages.shape
    dtype = section_pages.dtype
    query_count = query_rows.shape[0]
    return pl.pallas_call(
        pack_kernel,
        out_shape=(
            pltpu.HBM((insts, CAP * rows + query_count, head_dim), dtype),
            pltpu.HBM((insts, CAP * rows + query_count + STAT_ROWS, head_dim), dtype),
            pltpu.HBM((insts, query_count, head_dim), dtype),
        ),
        in_specs=[pl.BlockSpec(memory_space=pl.ANY)] * 3,
        out_specs=[pl.BlockSpec(memory_space=pl.ANY)] * 3,
        scratch_shapes=[
            pltpu.SMEM(spill_to.shape, jnp.int32),
            pltpu.SMEM(spill_to.shape, jnp.int32),
            pltpu.SMEM((insts,), jnp.int32),
            pltpu.VMEM(section_pages.shape, dtype),
            pltpu.VMEM((rows, head_dim), dtype),
            pltpu.VMEM(query_rows.shape, dtype),
            pltpu.VMEM((insts,) + query_rows.shape, dtype),
            pltpu.SemaphoreType.DMA((5,)),
        ],
        compiler_params=pltpu.CompilerParams(vmem_limit_bytes=4 * MIB),
        name="pack",
    )(in_hbm(spill_to), in_hbm(section_pages), in_hbm(query_rows))


def resident_kernel(score_scale, staged, owner_ref, arrived_ref, near_ref, far_ref, *others):
    if staged:
        *others, asked, near, sems = others
        query_count = asked.shape[1]
        first_query = arrived_ref.shape[1] - query_count
        copies = [
            pltpu.make_async_copy(arrived_ref.at[:, pl.ds(first_query, query_count)], asked, sems.at[0]),
            pltpu.make_async_copy(near_ref.at[:, 0], near.at[:, 0], sems.at[1]),
            pltpu.make_async_copy(near_ref.at[:, 1], near.at[:, 1], sems.at[2]),
        ]
        for copy in copies:
            copy.start()
        arrived_ref, near_ref = asked, near
    out_ref, partials, score, top, total, mix, part_sem = others[-7:]
    requests, query_count = mix.shape[0], mix.shape[1]
    slots = near_ref.shape[0]
    top[...] = jnp.full(top.shape, NEG, jnp.float32)
    total[...] = jnp.zeros_like(total)
    mix[...] = jnp.zeros_like(mix)

    if staged:
        copies[0].wait()
        copies[1].wait()
    for slot in range(slots):
        owner = owner_ref[slot]
        keys = jnp.concatenate([near_ref[slot, 0], far_ref[slot, 0]], axis=0)
        found = lax.dot_general(arrived_ref[owner], keys, NT, preferred_element_type=jnp.float32) * score_scale
        score[slot] = found
        top[owner] = jnp.maximum(top[owner], found)

    for request in range(requests):
        top[request] = jnp.broadcast_to(jnp.max(top[request], axis=1, keepdims=True), top.shape[1:])
    if staged:
        copies[2].wait()
    for slot in range(slots):
        owner = owner_ref[slot]
        weights = jnp.exp(score[slot] - top[owner])
        values = jnp.concatenate([near_ref[slot, 1], far_ref[slot, 1]], axis=0)
        total[owner] = total[owner] + weights
        mix[owner] = mix[owner] + jnp.dot(
            weights.astype(jnp.bfloat16), values, preferred_element_type=jnp.float32
        )
    gap = lax.broadcasted_iota(jnp.int32, top.shape[1:], 1) - lax.broadcasted_iota(jnp.int32, top.shape[1:], 0)
    stat_rows = partials.shape[1] - query_count
    for request in range(requests):
        norm = jnp.sum(total[request], axis=1, keepdims=True)
        held = norm > 0.0
        safe = jnp.where(held, norm, 1.0)
        partials[request, 0:query_count] = (mix[request] / safe).astype(jnp.bfloat16)
        level = jnp.where(held, top[request] + jnp.log(safe), NEG)
        high = level.astype(jnp.bfloat16).astype(jnp.float32)
        middle = (level - high).astype(jnp.bfloat16).astype(jnp.float32)
        low = level - high - middle
        terms = jnp.where(
            gap == 0, high, jnp.where(gap == query_count, middle, jnp.where(gap == 2 * query_count, low, 0.0))
        )
        terms = jnp.sum(terms, axis=0, keepdims=True)
        partials[request, query_count:] = jnp.broadcast_to(terms, (stat_rows, terms.shape[1])).astype(jnp.bfloat16)
    part_rows = partials.shape[1]
    part_copy = pltpu.make_async_copy(
        partials, out_ref.at[:, pl.ds(out_ref.shape[1] - part_rows, part_rows)], part_sem
    )
    part_copy.start()
    part_copy.wait()


def resident(owner_of, arrived, near, far, outgoing, score_scale, query_count):
    requests, head_dim = arrived.shape[0], arrived.shape[2]
    slots, tokens = near.shape[0], 2 * near.shape[2]
    part_rows = query_count + STAT_ROWS
    out_shape, aliases = (requests, part_rows, head_dim), {}
    staged = outgoing is None
    scratch = [
        pltpu.VMEM((requests, part_rows, head_dim), arrived.dtype),
        pltpu.VMEM((slots, query_count, tokens), jnp.float32),
        pltpu.VMEM((requests, query_count, tokens), jnp.float32),
        pltpu.VMEM((requests, query_count, tokens), jnp.float32),
        pltpu.VMEM((requests, query_count, head_dim), jnp.float32),
        pltpu.SemaphoreType.DMA,
    ]
    if staged:
        operands = [owner_of, arrived, in_hbm(near), in_vmem(far)]
        spaces = [pltpu.SMEM, pl.ANY, pl.ANY, pltpu.VMEM]
        scratch += [
            pltpu.VMEM((requests, query_count, head_dim), arrived.dtype),
            pltpu.VMEM(near.shape, near.dtype),
            pltpu.SemaphoreType.DMA((3,)),
        ]
    else:
        out_shape, aliases = outgoing.shape, {4: 0}
        operands = [owner_of, in_vmem(arrived), in_vmem(near), in_vmem(far), in_hbm(outgoing)]
        spaces = [pltpu.SMEM] + [pltpu.VMEM] * 3 + [pl.ANY]
    return pl.pallas_call(
        functools.partial(resident_kernel, score_scale, staged),
        out_shape=pltpu.HBM(out_shape, arrived.dtype),
        in_specs=[pl.BlockSpec(memory_space=space) for space in spaces],
        out_specs=pl.BlockSpec(memory_space=pl.ANY),
        scratch_shapes=scratch,
        input_output_aliases=aliases,
        compiler_params=pltpu.CompilerParams(vmem_limit_bytes=8 * MIB),
        name="resident_staged" if staged else "resident",
    )(*operands)


def own_kernel(score_scale, place_ref, query_ref, near_ref, far_ref, fresh_ref, out_ref):
    length, near_half = place_ref[0], place_ref[1]
    query_rows = query_ref[...]
    query_count, head_dim = query_rows.shape
    sectioned, half_len = near_ref.shape[0], near_ref.shape[2]
    first_page = (length + PAGE - 1) // PAGE - sectioned
    column = lax.broadcasted_iota(jnp.int32, (query_count, sectioned * half_len), 1)
    base = first_page * PAGE + column // half_len * PAGE + column % half_len
    scores, masks = [], []
    for half_ref, half in ((near_ref, near_half), (far_ref, 1 - near_half)):
        keys = half_ref[:, 0].reshape(sectioned * half_len, head_dim)
        found = lax.dot_general(query_rows, keys, NT, preferred_element_type=jnp.float32) * score_scale
        masks.append(base + half * half_len < length)
        scores.append(found)
    found = lax.dot_general(query_rows, fresh_ref[0], NT, preferred_element_type=jnp.float32) * score_scale
    step = lax.broadcasted_iota(jnp.int32, found.shape, 0) // (query_count // NEW)
    token = lax.broadcasted_iota(jnp.int32, found.shape, 1)
    masks.append(token <= step)
    scores.append(found)
    scores = [jnp.where(mask, found, NEG) for mask, found in zip(masks, scores, strict=True)]
    top = functools.reduce(jnp.maximum, [jnp.max(found, axis=1, keepdims=True) for found in scores])
    weights = [jnp.where(mask, jnp.exp(found - top), 0.0) for mask, found in zip(masks, scores, strict=True)]
    total = sum(jnp.sum(weight, axis=1, keepdims=True) for weight in weights)
    values = [
        near_ref[:, 1].reshape(sectioned * half_len, head_dim),
        far_ref[:, 1].reshape(sectioned * half_len, head_dim),
        fresh_ref[1],
    ]
    out_ref[0] = sum(
        jnp.dot(weight.astype(jnp.bfloat16), value, preferred_element_type=jnp.float32)
        for weight, value in zip(weights, values, strict=True)
    )
    out_ref[1] = jnp.broadcast_to(total, (query_count, head_dim))
    out_ref[2] = jnp.broadcast_to(top, (query_count, head_dim))


def own_partial(place, query_rows, near, far, fresh, score_scale):
    return pl.pallas_call(
        functools.partial(own_kernel, score_scale),
        out_shape=jax.ShapeDtypeStruct((3,) + query_rows.shape, jnp.float32),
        in_specs=[pl.BlockSpec(memory_space=pltpu.SMEM)] + [pl.BlockSpec(memory_space=pltpu.VMEM)] * 4,
        out_specs=pl.BlockSpec(memory_space=pltpu.VMEM),
        compiler_params=pltpu.CompilerParams(vmem_limit_bytes=16 * MIB),
        name="own_pages",
    )(place, query_rows, near, far, fresh)


def lend_kernel(arrived_ref, lent_ref, pages, sems):
    pieces = sems.shape[0] // 2
    count = lent_ref.shape[0] // pieces
    arriving, leaving = [], []
    for piece in range(pieces):
        part = pl.ds(piece * count, count)
        arriving.append(
            pltpu.make_async_copy(
                arrived_ref.at[part, pl.ds(0, lent_ref.shape[1])], pages.at[part], sems.at[2 * piece]
            )
        )
        leaving.append(pltpu.make_async_copy(pages.at[part], lent_ref.at[part], sems.at[2 * piece + 1]))
        arriving[-1].start()
    for into, out in zip(arriving, leaving, strict=True):
        into.wait()
        out.start()
    for out in leaving:
        out.wait()


def lend(arrived, page_rows):
    insts, head_dim = arrived.shape[0], arrived.shape[2]
    return pl.pallas_call(
        lend_kernel,
        out_shape=pltpu.HBM((insts, page_rows, head_dim), arrived.dtype),
        in_specs=[pl.BlockSpec(memory_space=pl.ANY)],
        out_specs=pl.BlockSpec(memory_space=pl.ANY),
        scratch_shapes=[
            pltpu.VMEM((insts, page_rows, head_dim), arrived.dtype),
            pltpu.SemaphoreType.DMA((8,)),
        ],
        compiler_params=pltpu.CompilerParams(vmem_limit_bytes=4 * MIB),
        name="lend",
    )(arrived)


def join(arrived_ref, own_ref, out_ref, own, own_sem):
    query_count, head_dim = out_ref.shape
    first_row = arrived_ref.shape[1] - query_count - STAT_ROWS
    own_copy = pltpu.make_async_copy(own_ref, own, own_sem)
    own_copy.start()
    outs = arrived_ref[:, first_row : first_row + query_count].astype(jnp.float32)
    terms = arrived_ref[:, first_row + query_count :].astype(jnp.float32)[:, 0:1]
    shape = (query_count, head_dim)
    lane = lax.broadcasted_iota(jnp.int32, shape, 1)
    own_lane = (lane % query_count == lax.broadcasted_iota(jnp.int32, shape, 0)) & (lane < 3 * query_count)
    levels = jnp.sum(jnp.where(own_lane[None], terms, 0.0), axis=2, keepdims=True)
    own_copy.wait()
    own_mix, own_total, own_top = own[0], own[1], own[2]
    joint = jnp.maximum(jnp.max(levels, axis=0), own_top)
    factor = jnp.exp(levels - joint[None])
    own_factor = jnp.exp(own_top - joint)
    norm = jnp.sum(factor, axis=0) + own_total * own_factor
    mixture = jnp.sum(outs * factor, axis=0) + own_mix * own_factor
    out_ref[...] = (mixture / norm).astype(jnp.bfloat16)


def finish_kernel(arrived_ref, own_ref, out_ref, lent_ref, own, own_sem, lent_sem):
    lent_copy = pltpu.make_async_copy(arrived_ref.at[:, pl.ds(0, lent_ref.shape[1])], lent_ref, lent_sem)
    lent_copy.start()
    join(arrived_ref, own_ref, out_ref, own, own_sem)
    lent_copy.wait()


def finish(arrived, own, page_rows):
    insts, head_dim = arrived.shape[0], arrived.shape[2]
    attended = jax.ShapeDtypeStruct(own.shape[1:], jnp.bfloat16)
    scratch = [pltpu.VMEM(own.shape, own.dtype), pltpu.SemaphoreType.DMA]
    in_place = pl.BlockSpec(memory_space=pl.ANY)
    if page_rows:
        attended = (attended, pltpu.HBM((insts, page_rows, head_dim), arrived.dtype))
        scratch.append(pltpu.SemaphoreType.DMA)
    return pl.pallas_call(
        finish_kernel if page_rows else join,
        out_shape=attended,
        in_specs=[pl.BlockSpec(memory_space=pltpu.VMEM), in_place],
        out_specs=(pl.BlockSpec(memory_space=pltpu.VMEM), in_place)
        if page_rows
        else pl.BlockSpec(memory_space=pltpu.VMEM),
        scratch_shapes=scratch,
        compiler_params=pltpu.CompilerParams(vmem_limit_bytes=8 * MIB),
        name="finish" if page_rows else "join",
    )(in_vmem(arrived), in_hbm(own))


def shards(pool, sectioning, spill_to, tables, lengths, queries, new_kv):
    insts = lax.axis_size("inst")
    resident_slots, half_len, head_dim = pool.shape[0], pool.shape[3], pool.shape[4]
    sectioned = sectioning.shape[0]
    steps = queries.shape[1]
    query_count = steps * queries.shape[2]
    score_scale = head_dim ** (-0.5)
    query_rows = queries.reshape(query_count, head_dim)

    section_pages = sectioning.reshape(sectioned, 2 * half_len, head_dim)
    page_rows = CAP * 2 * half_len
    near_pool = pool.reshape(resident_slots, 2, half_len, head_dim)
    near_section = sectioning.reshape(sectioned, 2, half_len, head_dim)
    far_pool = lax.ppermute(near_pool, "core", [(0, 1), (1, 0)])
    far_section = lax.ppermute(near_section, "core", [(0, 1), (1, 0)])
    whole, paged, asking = pack(spill_to, section_pages, query_rows, insts)

    def exchange(outgoing):
        return lax.all_to_all(outgoing, "inst", split_axis=0, concat_axis=0, tiled=True)

    def owners():
        held_here = (tables[:, :, 0] == lax.axis_index("inst"))[:, :, None] & (
            tables[:, :, 1][:, :, None] == jnp.arange(resident_slots, dtype=jnp.int32)
        )
        request_ids = jnp.arange(tables.shape[0], dtype=jnp.int32)
        return jnp.sum(jnp.where(held_here, request_ids[:, None, None], 0), axis=(0, 1))

    def own_part(far_section):
        length = lax.dynamic_index_in_dim(lengths, lax.axis_index("inst"), 0, keepdims=False)
        place = jnp.stack([length, lax.axis_index("core").astype(jnp.int32)])
        fresh = lax.dynamic_slice_in_dim(new_kv[0], lax.axis_index("pair"), 1, 2)[:, :, 0]
        fresh = jnp.pad(jnp.swapaxes(fresh, 0, 1), ((0, 0), (0, query_count - steps), (0, 0)))
        return own_partial(place, query_rows, near_section, far_section, fresh, score_scale)

    def queries_first(whole, paged, asking, far_pool, far_section):
        asked = exchange(asking)
        own = own_part(far_section)
        paged = resident(owners(), asked, near_pool, far_pool, paged, score_scale, query_count)
        return finish(exchange(paged), own, page_rows)

    def pages_first(whole, paged, asking, far_pool, far_section):
        arrived = exchange(whole)
        own = own_part(far_section)
        partials = resident(owners(), arrived, near_pool, far_pool, None, score_scale, query_count)
        lent = lend(arrived, page_rows)
        return finish(exchange(partials), own, 0), lent

    attended, lent = lax.cond(
        lax.axis_index("core") == 0, queries_first, pages_first, whole, paged, asking, far_pool, far_section
    )
    return attended.reshape(queries.shape), lent.reshape(insts * CAP, 1, 2, half_len, head_dim)


def solution(mesh):
    insts, tp = mesh.devices.shape
    paired = Mesh(mesh.devices.reshape(insts, tp // 2, 2), ("inst", "pair", "core"))
    heads = ("pair", "core")
    return jax.shard_map(
        shards,
        mesh=paired,
        in_specs=(
            P("inst", heads),
            P("inst", heads),
            P("inst"),
            P(),
            P(),
            P("inst", None, heads),
            P("inst"),
        ),
        out_specs=(P("inst", None, heads), P("inst", heads)),
        check_vma=False,
    )
```

```python
import functools

import jax
import jax.numpy as jnp
from jax import lax
from jax.experimental import pallas as pl
from jax.experimental.pallas import tpu as pltpu
from jax.sharding import Mesh, PartitionSpec as P

PAGE = 128
CAP = 2
NEG = -1e30
NEW = 4
STAT_ROWS = 16
MIB = 1024 * 1024
NT = (((1,), (1,)), ((), ()))


def in_vmem(value):
    return pltpu.with_memory_space_constraint(value, pltpu.VMEM)


def in_hbm(value):
    return pltpu.with_memory_space_constraint(value, pltpu.HBM)


def pack_kernel(
    spill_ref,
    section_ref,
    query_ref,
    whole_ref,
    paged_ref,
    asking_ref,
    spill,
    place,
    count,
    pages,
    zeros,
    asked,
    spread,
    sems,
):
    insts = whole_ref.shape[0]
    sectioned, rows = section_ref.shape[0], section_ref.shape[1]
    core = lax.axis_index("core")
    spill_copy = pltpu.make_async_copy(spill_ref, spill, sems.at[0])
    page_copy = pltpu.make_async_copy(section_ref, pages, sems.at[1])
    query_copy = pltpu.make_async_copy(query_ref, asked, sems.at[2])
    spill_copy.start()
    query_copy.start()
    page_copy.start()
    zeros[...] = jnp.zeros_like(zeros)
    for dest in range(insts):
        count[dest] = 0
    spill_copy.wait()

    @pl.loop(0, sectioned)
    def _(row):
        dest = spill[row]
        place[row] = count[dest]
        count[dest] = count[dest] + 1

    def lay_out(out_ref, query_rows_ref):
        def slot_copy(source, dest, rank):
            start = pl.multiple_of(rank * rows, rows)
            return pltpu.make_async_copy(source, out_ref.at[dest, pl.ds(start, rows)], sems.at[3])

        @pl.loop(0, insts)
        def _(dest):
            filled = count[dest]
            for rank in range(CAP):

                @pl.when(filled <= rank)
                def _():
                    slot_copy(zeros, dest, rank).start()

        query_copy.wait()
        spread[...] = jnp.broadcast_to(asked[...][None], spread.shape)
        spread_copy = pltpu.make_async_copy(spread, query_rows_ref, sems.at[4])
        spread_copy.start()
        page_copy.wait()

        @pl.loop(0, sectioned)
        def _(row):
            slot_copy(pages.at[row], spill[row], place[row]).start()

        all_slots = out_ref.at[:, pl.ds(0, CAP * rows)]
        pltpu.make_async_copy(all_slots, all_slots, sems.at[3]).wait()
        spread_copy.wait()

    @pl.when(core == 1)
    def _():
        lay_out(whole_ref, whole_ref.at[:, pl.ds(CAP * rows, asked.shape[0])])

    @pl.when(core == 0)
    def _():
        lay_out(paged_ref, asking_ref)


def pack(spill_to, section_pages, query_rows, insts):
    sectioned, rows, head_dim = section_pages.shape
    dtype = section_pages.dtype
    query_count = query_rows.shape[0]
    return pl.pallas_call(
        pack_kernel,
        out_shape=(
            pltpu.HBM((insts, CAP * rows + query_count, head_dim), dtype),
            pltpu.HBM((insts, CAP * rows + query_count + STAT_ROWS, head_dim), dtype),
            pltpu.HBM((insts, query_count, head_dim), dtype),
        ),
        in_specs=[pl.BlockSpec(memory_space=pl.ANY)] * 3,
        out_specs=[pl.BlockSpec(memory_space=pl.ANY)] * 3,
        scratch_shapes=[
            pltpu.SMEM(spill_to.shape, jnp.int32),
            pltpu.SMEM(spill_to.shape, jnp.int32),
            pltpu.SMEM((insts,), jnp.int32),
            pltpu.VMEM(section_pages.shape, dtype),
            pltpu.VMEM((rows, head_dim), dtype),
            pltpu.VMEM(query_rows.shape, dtype),
            pltpu.VMEM((insts,) + query_rows.shape, dtype),
            pltpu.SemaphoreType.DMA((5,)),
        ],
        compiler_params=pltpu.CompilerParams(vmem_limit_bytes=4 * MIB),
        name="pack",
    )(in_hbm(spill_to), in_hbm(section_pages), in_hbm(query_rows))


def resident_kernel(score_scale, staged, owner_ref, arrived_ref, near_ref, far_ref, *others):
    if staged:
        *others, asked, near, sems = others
        first_query = arrived_ref.shape[1] - asked.shape[1]
        asked_copy = pltpu.make_async_copy(
            arrived_ref.at[:, pl.ds(first_query, asked.shape[1])], asked, sems.at[2]
        )
        asked_copy.start()
    else:
        *others, near, sems = others
    key_copy = pltpu.make_async_copy(near_ref.at[:, 0], near.at[:, 0], sems.at[0])
    value_copy = pltpu.make_async_copy(near_ref.at[:, 1], near.at[:, 1], sems.at[1])
    key_copy.start()
    value_copy.start()
    near_ref = near
    out_ref, partials, score, top, total, mix, part_sem = others[-7:]
    requests, query_count = mix.shape[0], mix.shape[1]
    slots = near_ref.shape[0]
    top[...] = jnp.full(top.shape, NEG, jnp.float32)
    total[...] = jnp.zeros_like(total)
    mix[...] = jnp.zeros_like(mix)

    half_len = near_ref.shape[2]
    if staged:
        asked_copy.wait()
        arrived_ref = asked

    def scores(slot, keys):
        asked_rows = arrived_ref[owner_ref[slot]]
        return lax.dot_general(asked_rows, keys, NT, preferred_element_type=jnp.float32) * score_scale

    for slot in range(slots):
        score[slot, :, half_len:] = scores(slot, far_ref[slot, 0])
    key_copy.wait()
    for slot in range(slots):
        owner = owner_ref[slot]
        score[slot, :, :half_len] = scores(slot, near_ref[slot, 0])
        top[owner] = jnp.maximum(top[owner], score[slot])
    for request in range(requests):
        top[request] = jnp.broadcast_to(jnp.max(top[request], axis=1, keepdims=True), top.shape[1:])
    value_copy.wait()
    for slot in range(slots):
        owner = owner_ref[slot]
        weights = jnp.exp(score[slot] - top[owner])
        values = jnp.concatenate([near_ref[slot, 1], far_ref[slot, 1]], axis=0)
        total[owner] = total[owner] + weights
        mix[owner] = mix[owner] + jnp.dot(
            weights.astype(jnp.bfloat16), values, preferred_element_type=jnp.float32
        )
    gap = lax.broadcasted_iota(jnp.int32, top.shape[1:], 1) - lax.broadcasted_iota(jnp.int32, top.shape[1:], 0)
    stat_rows = partials.shape[1] - query_count
    for request in range(requests):
        norm = jnp.sum(total[request], axis=1, keepdims=True)
        held = norm > 0.0
        safe = jnp.where(held, norm, 1.0)
        partials[request, 0:query_count] = (mix[request] / safe).astype(jnp.bfloat16)
        level = jnp.where(held, top[request] + jnp.log(safe), NEG)
        high = level.astype(jnp.bfloat16).astype(jnp.float32)
        middle = (level - high).astype(jnp.bfloat16).astype(jnp.float32)
        low = level - high - middle
        terms = jnp.where(
            gap == 0, high, jnp.where(gap == query_count, middle, jnp.where(gap == 2 * query_count, low, 0.0))
        )
        terms = jnp.sum(terms, axis=0, keepdims=True)
        partials[request, query_count:] = jnp.broadcast_to(terms, (stat_rows, terms.shape[1])).astype(jnp.bfloat16)
    part_rows = partials.shape[1]
    part_copy = pltpu.make_async_copy(
        partials, out_ref.at[:, pl.ds(out_ref.shape[1] - part_rows, part_rows)], part_sem
    )
    part_copy.start()
    part_copy.wait()


def resident(owner_of, arrived, near, far, outgoing, score_scale, query_count):
    requests, head_dim = arrived.shape[0], arrived.shape[2]
    slots, tokens = near.shape[0], 2 * near.shape[2]
    part_rows = query_count + STAT_ROWS
    out_shape, aliases = (requests, part_rows, head_dim), {}
    staged = outgoing is None
    scratch = [
        pltpu.VMEM((requests, part_rows, head_dim), arrived.dtype),
        pltpu.VMEM((slots, query_count, tokens), jnp.float32),
        pltpu.VMEM((requests, query_count, tokens), jnp.float32),
        pltpu.VMEM((requests, query_count, tokens), jnp.float32),
        pltpu.VMEM((requests, query_count, head_dim), jnp.float32),
        pltpu.SemaphoreType.DMA,
    ]
    if staged:
        operands = [owner_of, arrived, in_hbm(near), in_vmem(far)]
        spaces = [pltpu.SMEM, pl.ANY, pl.ANY, pltpu.VMEM]
        scratch.append(pltpu.VMEM((requests, query_count, head_dim), arrived.dtype))
    else:
        out_shape, aliases = outgoing.shape, {4: 0}
        operands = [owner_of, in_vmem(arrived), in_hbm(near), in_vmem(far), in_hbm(outgoing)]
        spaces = [pltpu.SMEM, pltpu.VMEM, pl.ANY, pltpu.VMEM, pl.ANY]
    scratch += [pltpu.VMEM(near.shape, near.dtype), pltpu.SemaphoreType.DMA((3,))]
    return pl.pallas_call(
        functools.partial(resident_kernel, score_scale, staged),
        out_shape=pltpu.HBM(out_shape, arrived.dtype),
        in_specs=[pl.BlockSpec(memory_space=space) for space in spaces],
        out_specs=pl.BlockSpec(memory_space=pl.ANY),
        scratch_shapes=scratch,
        input_output_aliases=aliases,
        compiler_params=pltpu.CompilerParams(vmem_limit_bytes=8 * MIB),
        name="resident_staged" if staged else "resident",
    )(*operands)


def own_kernel(score_scale, place_ref, query_ref, near_ref, far_ref, fresh_ref, out_ref):
    length, near_half = place_ref[0], place_ref[1]
    query_rows = query_ref[...]
    query_count, head_dim = query_rows.shape
    sectioned, half_len = near_ref.shape[0], near_ref.shape[2]
    first_page = (length + PAGE - 1) // PAGE - sectioned
    column = lax.broadcasted_iota(jnp.int32, (query_count, sectioned * half_len), 1)
    base = first_page * PAGE + column // half_len * PAGE + column % half_len
    scores, masks = [], []
    for half_ref, half in ((near_ref, near_half), (far_ref, 1 - near_half)):
        keys = half_ref[:, 0].reshape(sectioned * half_len, head_dim)
        found = lax.dot_general(query_rows, keys, NT, preferred_element_type=jnp.float32) * score_scale
        masks.append(base + half * half_len < length)
        scores.append(found)
    found = lax.dot_general(query_rows, fresh_ref[0], NT, preferred_element_type=jnp.float32) * score_scale
    step = lax.broadcasted_iota(jnp.int32, found.shape, 0) // (query_count // NEW)
    token = lax.broadcasted_iota(jnp.int32, found.shape, 1)
    masks.append(token <= step)
    scores.append(found)
    scores = [jnp.where(mask, found, NEG) for mask, found in zip(masks, scores, strict=True)]
    top = functools.reduce(jnp.maximum, [jnp.max(found, axis=1, keepdims=True) for found in scores])
    weights = [jnp.where(mask, jnp.exp(found - top), 0.0) for mask, found in zip(masks, scores, strict=True)]
    total = sum(jnp.sum(weight, axis=1, keepdims=True) for weight in weights)
    values = [
        near_ref[:, 1].reshape(sectioned * half_len, head_dim),
        far_ref[:, 1].reshape(sectioned * half_len, head_dim),
        fresh_ref[1],
    ]
    out_ref[0] = sum(
        jnp.dot(weight.astype(jnp.bfloat16), value, preferred_element_type=jnp.float32)
        for weight, value in zip(weights, values, strict=True)
    )
    out_ref[1] = jnp.broadcast_to(total, (query_count, head_dim))
    out_ref[2] = jnp.broadcast_to(top, (query_count, head_dim))


def own_partial(place, query_rows, near, far, fresh, score_scale):
    return pl.pallas_call(
        functools.partial(own_kernel, score_scale),
        out_shape=jax.ShapeDtypeStruct((3,) + query_rows.shape, jnp.float32),
        in_specs=[pl.BlockSpec(memory_space=pltpu.SMEM)] + [pl.BlockSpec(memory_space=pltpu.VMEM)] * 4,
        out_specs=pl.BlockSpec(memory_space=pltpu.VMEM),
        compiler_params=pltpu.CompilerParams(vmem_limit_bytes=16 * MIB),
        name="own_pages",
    )(place, query_rows, near, far, fresh)


def lend_kernel(arrived_ref, lent_ref, pages, sems):
    pieces = sems.shape[0] // 2
    count = lent_ref.shape[0] // pieces
    arriving, leaving = [], []
    for piece in range(pieces):
        part = pl.ds(piece * count, count)
        arriving.append(
            pltpu.make_async_copy(
                arrived_ref.at[part, pl.ds(0, lent_ref.shape[1])], pages.at[part], sems.at[2 * piece]
            )
        )
        leaving.append(pltpu.make_async_copy(pages.at[part], lent_ref.at[part], sems.at[2 * piece + 1]))
        arriving[-1].start()
    for into, out in zip(arriving, leaving, strict=True):
        into.wait()
        out.start()
    for out in leaving:
        out.wait()


def lend(arrived, page_rows):
    insts, head_dim = arrived.shape[0], arrived.shape[2]
    return pl.pallas_call(
        lend_kernel,
        out_shape=pltpu.HBM((insts, page_rows, head_dim), arrived.dtype),
        in_specs=[pl.BlockSpec(memory_space=pl.ANY)],
        out_specs=pl.BlockSpec(memory_space=pl.ANY),
        scratch_shapes=[
            pltpu.VMEM((insts, page_rows, head_dim), arrived.dtype),
            pltpu.SemaphoreType.DMA((8,)),
        ],
        compiler_params=pltpu.CompilerParams(vmem_limit_bytes=4 * MIB),
        name="lend",
    )(arrived)


def join(arrived_ref, own_ref, out_ref, own, own_sem):
    query_count, head_dim = out_ref.shape
    first_row = arrived_ref.shape[1] - query_count - STAT_ROWS
    own_copy = pltpu.make_async_copy(own_ref, own, own_sem)
    own_copy.start()
    outs = arrived_ref[:, first_row : first_row + query_count].astype(jnp.float32)
    terms = arrived_ref[:, first_row + query_count :].astype(jnp.float32)[:, 0:1]
    shape = (query_count, head_dim)
    lane = lax.broadcasted_iota(jnp.int32, shape, 1)
    own_lane = (lane % query_count == lax.broadcasted_iota(jnp.int32, shape, 0)) & (lane < 3 * query_count)
    levels = jnp.sum(jnp.where(own_lane[None], terms, 0.0), axis=2, keepdims=True)
    own_copy.wait()
    own_mix, own_total, own_top = own[0], own[1], own[2]
    joint = jnp.maximum(jnp.max(levels, axis=0), own_top)
    factor = jnp.exp(levels - joint[None])
    own_factor = jnp.exp(own_top - joint)
    norm = jnp.sum(factor, axis=0) + own_total * own_factor
    mixture = jnp.sum(outs * factor, axis=0) + own_mix * own_factor
    out_ref[...] = (mixture / norm).astype(jnp.bfloat16)


def finish_kernel(arrived_ref, own_ref, out_ref, lent_ref, own, own_sem, lent_sem):
    lent_copy = pltpu.make_async_copy(arrived_ref.at[:, pl.ds(0, lent_ref.shape[1])], lent_ref, lent_sem)
    lent_copy.start()
    join(arrived_ref, own_ref, out_ref, own, own_sem)
    lent_copy.wait()


def finish(arrived, own, page_rows):
    insts, head_dim = arrived.shape[0], arrived.shape[2]
    attended = jax.ShapeDtypeStruct(own.shape[1:], jnp.bfloat16)
    scratch = [pltpu.VMEM(own.shape, own.dtype), pltpu.SemaphoreType.DMA]
    in_place = pl.BlockSpec(memory_space=pl.ANY)
    if page_rows:
        attended = (attended, pltpu.HBM((insts, page_rows, head_dim), arrived.dtype))
        scratch.append(pltpu.SemaphoreType.DMA)
    return pl.pallas_call(
        finish_kernel if page_rows else join,
        out_shape=attended,
        in_specs=[pl.BlockSpec(memory_space=pltpu.VMEM), in_place],
        out_specs=(pl.BlockSpec(memory_space=pltpu.VMEM), in_place)
        if page_rows
        else pl.BlockSpec(memory_space=pltpu.VMEM),
        scratch_shapes=scratch,
        compiler_params=pltpu.CompilerParams(vmem_limit_bytes=8 * MIB),
        name="finish" if page_rows else "join",
    )(in_vmem(arrived), in_hbm(own))


def shards(pool, sectioning, spill_to, tables, lengths, queries, new_kv):
    insts = lax.axis_size("inst")
    resident_slots, half_len, head_dim = pool.shape[0], pool.shape[3], pool.shape[4]
    sectioned = sectioning.shape[0]
    steps = queries.shape[1]
    query_count = steps * queries.shape[2]
    score_scale = head_dim ** (-0.5)
    query_rows = queries.reshape(query_count, head_dim)

    section_pages = sectioning.reshape(sectioned, 2 * half_len, head_dim)
    page_rows = CAP * 2 * half_len
    near_pool = pool.reshape(resident_slots, 2, half_len, head_dim)
    near_section = sectioning.reshape(sectioned, 2, half_len, head_dim)
    far_pool = lax.ppermute(near_pool, "core", [(0, 1), (1, 0)])
    far_section = lax.ppermute(near_section, "core", [(0, 1), (1, 0)])
    whole, paged, asking = pack(spill_to, section_pages, query_rows, insts)

    def exchange(outgoing):
        return lax.all_to_all(outgoing, "inst", split_axis=0, concat_axis=0, tiled=True)

    def owners():
        held_here = (tables[:, :, 0] == lax.axis_index("inst"))[:, :, None] & (
            tables[:, :, 1][:, :, None] == jnp.arange(resident_slots, dtype=jnp.int32)
        )
        request_ids = jnp.arange(tables.shape[0], dtype=jnp.int32)
        return jnp.sum(jnp.where(held_here, request_ids[:, None, None], 0), axis=(0, 1))

    def own_part(far_section):
        length = lax.dynamic_index_in_dim(lengths, lax.axis_index("inst"), 0, keepdims=False)
        place = jnp.stack([length, lax.axis_index("core").astype(jnp.int32)])
        fresh = lax.dynamic_slice_in_dim(new_kv[0], lax.axis_index("pair"), 1, 2)[:, :, 0]
        fresh = jnp.pad(jnp.swapaxes(fresh, 0, 1), ((0, 0), (0, query_count - steps), (0, 0)))
        return own_partial(place, query_rows, near_section, far_section, fresh, score_scale)

    def queries_first(whole, paged, asking, far_pool, far_section):
        asked = exchange(asking)
        own = own_part(far_section)
        paged = resident(owners(), asked, near_pool, far_pool, paged, score_scale, query_count)
        return finish(exchange(paged), own, page_rows)

    def pages_first(whole, paged, asking, far_pool, far_section):
        arrived = exchange(whole)
        own = own_part(far_section)
        partials = resident(owners(), arrived, near_pool, far_pool, None, score_scale, query_count)
        lent = lend(arrived, page_rows)
        return finish(exchange(partials), own, 0), lent

    attended, lent = lax.cond(
        lax.axis_index("core") == 0, queries_first, pages_first, whole, paged, asking, far_pool, far_section
    )
    return attended.reshape(queries.shape), lent.reshape(insts * CAP, 1, 2, half_len, head_dim)


def solution(mesh):
    insts, tp = mesh.devices.shape
    paired = Mesh(mesh.devices.reshape(insts, tp // 2, 2), ("inst", "pair", "core"))
    heads = ("pair", "core")
    return jax.shard_map(
        shards,
        mesh=paired,
        in_specs=(
            P("inst", heads),
            P("inst", heads),
            P("inst"),
            P(),
            P(),
            P("inst", None, heads),
            P("inst"),
        ),
        out_specs=(P("inst", None, heads), P("inst", heads)),
        check_vma=False,
    )
```

```python
import functools

import jax
import jax.numpy as jnp
from jax import lax
from jax.experimental import pallas as pl
from jax.experimental.pallas import tpu as pltpu
from jax.sharding import Mesh, PartitionSpec as P

PAGE = 128
CAP = 2
NEG = -1e30
NEW = 4
STAT_ROWS = 16
MIB = 1024 * 1024
NT = (((1,), (1,)), ((), ()))


def in_vmem(value):
    return pltpu.with_memory_space_constraint(value, pltpu.VMEM)


def in_hbm(value):
    return pltpu.with_memory_space_constraint(value, pltpu.HBM)


def pack_kernel(
    spill_ref,
    section_ref,
    query_ref,
    whole_ref,
    paged_ref,
    asking_ref,
    spill,
    place,
    count,
    zeros,
    asked,
    spread,
    sems,
):
    insts = whole_ref.shape[0]
    sectioned, rows = section_ref.shape[0], section_ref.shape[1]
    core = lax.axis_index("core")
    spill_copy = pltpu.make_async_copy(spill_ref, spill, sems.at[0])
    query_copy = pltpu.make_async_copy(query_ref, asked, sems.at[2])
    spill_copy.start()
    query_copy.start()
    zeros[...] = jnp.zeros_like(zeros)
    for dest in range(insts):
        count[dest] = 0
    spill_copy.wait()

    @pl.loop(0, sectioned)
    def _(row):
        dest = spill[row]
        place[row] = count[dest]
        count[dest] = count[dest] + 1

    def lay_out(out_ref, query_rows_ref):
        def slot_copy(source, dest, rank):
            start = pl.multiple_of(rank * rows, rows)
            return pltpu.make_async_copy(source, out_ref.at[dest, pl.ds(start, rows)], sems.at[3])

        @pl.loop(0, insts)
        def _(dest):
            filled = count[dest]
            for rank in range(CAP):

                @pl.when(filled <= rank)
                def _():
                    slot_copy(zeros, dest, rank).start()

        query_copy.wait()
        spread[...] = jnp.broadcast_to(asked[...][None], spread.shape)
        spread_copy = pltpu.make_async_copy(spread, query_rows_ref, sems.at[4])
        spread_copy.start()

        @pl.loop(0, sectioned)
        def _(row):
            slot_copy(section_ref.at[row], spill[row], place[row]).start()

        all_slots = out_ref.at[:, pl.ds(0, CAP * rows)]
        pltpu.make_async_copy(all_slots, all_slots, sems.at[3]).wait()
        spread_copy.wait()

    @pl.when(core == 1)
    def _():
        lay_out(whole_ref, whole_ref.at[:, pl.ds(CAP * rows, asked.shape[0])])

    @pl.when(core == 0)
    def _():
        lay_out(paged_ref, asking_ref)


def pack(spill_to, section_pages, query_rows, insts):
    sectioned, rows, head_dim = section_pages.shape
    dtype = section_pages.dtype
    query_count = query_rows.shape[0]
    return pl.pallas_call(
        pack_kernel,
        out_shape=(
            pltpu.HBM((insts, CAP * rows + query_count, head_dim), dtype),
            pltpu.HBM((insts, CAP * rows + query_count + STAT_ROWS, head_dim), dtype),
            pltpu.HBM((insts, query_count, head_dim), dtype),
        ),
        in_specs=[pl.BlockSpec(memory_space=space) for space in (pl.ANY, pltpu.VMEM, pl.ANY)],
        out_specs=[pl.BlockSpec(memory_space=pl.ANY)] * 3,
        scratch_shapes=[
            pltpu.SMEM(spill_to.shape, jnp.int32),
            pltpu.SMEM(spill_to.shape, jnp.int32),
            pltpu.SMEM((insts,), jnp.int32),
            pltpu.VMEM((rows, head_dim), dtype),
            pltpu.VMEM(query_rows.shape, dtype),
            pltpu.VMEM((insts,) + query_rows.shape, dtype),
            pltpu.SemaphoreType.DMA((5,)),
        ],
        compiler_params=pltpu.CompilerParams(vmem_limit_bytes=4 * MIB),
        name="pack",
    )(in_hbm(spill_to), in_vmem(section_pages), in_hbm(query_rows))


def resident_kernel(score_scale, staged, owner_ref, arrived_ref, near_ref, far_ref, *others):
    if staged:
        *others, asked, near, sems = others
        first_query = arrived_ref.shape[1] - asked.shape[1]
        asked_copy = pltpu.make_async_copy(
            arrived_ref.at[:, pl.ds(first_query, asked.shape[1])], asked, sems.at[2]
        )
        asked_copy.start()
    else:
        *others, near, sems = others
    key_copy = pltpu.make_async_copy(near_ref.at[:, 0], near.at[:, 0], sems.at[0])
    value_copy = pltpu.make_async_copy(near_ref.at[:, 1], near.at[:, 1], sems.at[1])
    key_copy.start()
    value_copy.start()
    near_ref = near
    out_ref, partials, score, top, total, mix, part_sem = others[-7:]
    requests, query_count = mix.shape[0], mix.shape[1]
    slots = near_ref.shape[0]
    top[...] = jnp.full(top.shape, NEG, jnp.float32)
    total[...] = jnp.zeros_like(total)
    mix[...] = jnp.zeros_like(mix)

    half_len = near_ref.shape[2]
    if staged:
        asked_copy.wait()
        arrived_ref = asked

    def scores(slot, keys):
        asked_rows = arrived_ref[owner_ref[slot]]
        return lax.dot_general(asked_rows, keys, NT, preferred_element_type=jnp.float32) * score_scale

    for slot in range(slots):
        score[slot, :, half_len:] = scores(slot, far_ref[slot, 0])
    key_copy.wait()
    for slot in range(slots):
        owner = owner_ref[slot]
        score[slot, :, :half_len] = scores(slot, near_ref[slot, 0])
        top[owner] = jnp.maximum(top[owner], score[slot])
    for request in range(requests):
        top[request] = jnp.broadcast_to(jnp.max(top[request], axis=1, keepdims=True), top.shape[1:])
    value_copy.wait()
    for slot in range(slots):
        owner = owner_ref[slot]
        weights = jnp.exp(score[slot] - top[owner])
        values = jnp.concatenate([near_ref[slot, 1], far_ref[slot, 1]], axis=0)
        total[owner] = total[owner] + weights
        mix[owner] = mix[owner] + jnp.dot(
            weights.astype(jnp.bfloat16), values, preferred_element_type=jnp.float32
        )
    gap = lax.broadcasted_iota(jnp.int32, top.shape[1:], 1) - lax.broadcasted_iota(jnp.int32, top.shape[1:], 0)
    stat_rows = partials.shape[1] - query_count
    for request in range(requests):
        norm = jnp.sum(total[request], axis=1, keepdims=True)
        held = norm > 0.0
        safe = jnp.where(held, norm, 1.0)
        partials[request, 0:query_count] = (mix[request] / safe).astype(jnp.bfloat16)
        level = jnp.where(held, top[request] + jnp.log(safe), NEG)
        high = level.astype(jnp.bfloat16).astype(jnp.float32)
        middle = (level - high).astype(jnp.bfloat16).astype(jnp.float32)
        low = level - high - middle
        terms = jnp.where(
            gap == 0, high, jnp.where(gap == query_count, middle, jnp.where(gap == 2 * query_count, low, 0.0))
        )
        terms = jnp.sum(terms, axis=0, keepdims=True)
        partials[request, query_count:] = jnp.broadcast_to(terms, (stat_rows, terms.shape[1])).astype(jnp.bfloat16)
    part_rows = partials.shape[1]
    part_copy = pltpu.make_async_copy(
        partials, out_ref.at[:, pl.ds(out_ref.shape[1] - part_rows, part_rows)], part_sem
    )
    part_copy.start()
    part_copy.wait()


def resident(owner_of, arrived, near, far, outgoing, score_scale, query_count):
    requests, head_dim = arrived.shape[0], arrived.shape[2]
    slots, tokens = near.shape[0], 2 * near.shape[2]
    part_rows = query_count + STAT_ROWS
    out_shape, aliases = (requests, part_rows, head_dim), {}
    staged = outgoing is None
    scratch = [
        pltpu.VMEM((requests, part_rows, head_dim), arrived.dtype),
        pltpu.VMEM((slots, query_count, tokens), jnp.float32),
        pltpu.VMEM((requests, query_count, tokens), jnp.float32),
        pltpu.VMEM((requests, query_count, tokens), jnp.float32),
        pltpu.VMEM((requests, query_count, head_dim), jnp.float32),
        pltpu.SemaphoreType.DMA,
    ]
    if staged:
        operands = [owner_of, arrived, in_hbm(near), in_vmem(far)]
        spaces = [pltpu.SMEM, pl.ANY, pl.ANY, pltpu.VMEM]
        scratch.append(pltpu.VMEM((requests, query_count, head_dim), arrived.dtype))
    else:
        out_shape, aliases = outgoing.shape, {4: 0}
        operands = [owner_of, in_vmem(arrived), in_hbm(near), in_vmem(far), in_hbm(outgoing)]
        spaces = [pltpu.SMEM, pltpu.VMEM, pl.ANY, pltpu.VMEM, pl.ANY]
    scratch += [pltpu.VMEM(near.shape, near.dtype), pltpu.SemaphoreType.DMA((3,))]
    return pl.pallas_call(
        functools.partial(resident_kernel, score_scale, staged),
        out_shape=pltpu.HBM(out_shape, arrived.dtype),
        in_specs=[pl.BlockSpec(memory_space=space) for space in spaces],
        out_specs=pl.BlockSpec(memory_space=pl.ANY),
        scratch_shapes=scratch,
        input_output_aliases=aliases,
        compiler_params=pltpu.CompilerParams(vmem_limit_bytes=8 * MIB),
        name="resident_staged" if staged else "resident",
    )(*operands)


def own_kernel(score_scale, place_ref, query_ref, near_ref, far_ref, fresh_ref, out_ref):
    length, near_half = place_ref[0], place_ref[1]
    query_rows = query_ref[...]
    query_count, head_dim = query_rows.shape
    sectioned, half_len = near_ref.shape[0], near_ref.shape[2]
    first_page = (length + PAGE - 1) // PAGE - sectioned
    column = lax.broadcasted_iota(jnp.int32, (query_count, sectioned * half_len), 1)
    base = first_page * PAGE + column // half_len * PAGE + column % half_len
    scores, masks = [], []
    for half_ref, half in ((near_ref, near_half), (far_ref, 1 - near_half)):
        keys = half_ref[:, 0].reshape(sectioned * half_len, head_dim)
        found = lax.dot_general(query_rows, keys, NT, preferred_element_type=jnp.float32) * score_scale
        masks.append(base + half * half_len < length)
        scores.append(found)
    found = lax.dot_general(query_rows, fresh_ref[0], NT, preferred_element_type=jnp.float32) * score_scale
    step = lax.broadcasted_iota(jnp.int32, found.shape, 0) // (query_count // NEW)
    token = lax.broadcasted_iota(jnp.int32, found.shape, 1)
    masks.append(token <= step)
    scores.append(found)
    scores = [jnp.where(mask, found, NEG) for mask, found in zip(masks, scores, strict=True)]
    top = functools.reduce(jnp.maximum, [jnp.max(found, axis=1, keepdims=True) for found in scores])
    weights = [jnp.where(mask, jnp.exp(found - top), 0.0) for mask, found in zip(masks, scores, strict=True)]
    total = sum(jnp.sum(weight, axis=1, keepdims=True) for weight in weights)
    values = [
        near_ref[:, 1].reshape(sectioned * half_len, head_dim),
        far_ref[:, 1].reshape(sectioned * half_len, head_dim),
        fresh_ref[1],
    ]
    out_ref[0] = sum(
        jnp.dot(weight.astype(jnp.bfloat16), value, preferred_element_type=jnp.float32)
        for weight, value in zip(weights, values, strict=True)
    )
    out_ref[1] = jnp.broadcast_to(total, (query_count, head_dim))
    out_ref[2] = jnp.broadcast_to(top, (query_count, head_dim))


def own_partial(place, query_rows, near, far, fresh, score_scale):
    return pl.pallas_call(
        functools.partial(own_kernel, score_scale),
        out_shape=jax.ShapeDtypeStruct((3,) + query_rows.shape, jnp.float32),
        in_specs=[pl.BlockSpec(memory_space=pltpu.SMEM)] + [pl.BlockSpec(memory_space=pltpu.VMEM)] * 4,
        out_specs=pl.BlockSpec(memory_space=pltpu.VMEM),
        compiler_params=pltpu.CompilerParams(vmem_limit_bytes=16 * MIB),
        name="own_pages",
    )(place, query_rows, near, far, fresh)


def lend_kernel(arrived_ref, lent_ref, pages, sems):
    pieces = sems.shape[0] // 2
    count = lent_ref.shape[0] // pieces
    arriving, leaving = [], []
    for piece in range(pieces):
        part = pl.ds(piece * count, count)
        arriving.append(
            pltpu.make_async_copy(
                arrived_ref.at[part, pl.ds(0, lent_ref.shape[1])], pages.at[part], sems.at[2 * piece]
            )
        )
        leaving.append(pltpu.make_async_copy(pages.at[part], lent_ref.at[part], sems.at[2 * piece + 1]))
        arriving[-1].start()
    for into, out in zip(arriving, leaving, strict=True):
        into.wait()
        out.start()
    for out in leaving:
        out.wait()


def lend(arrived, page_rows):
    insts, head_dim = arrived.shape[0], arrived.shape[2]
    return pl.pallas_call(
        lend_kernel,
        out_shape=pltpu.HBM((insts, page_rows, head_dim), arrived.dtype),
        in_specs=[pl.BlockSpec(memory_space=pl.ANY)],
        out_specs=pl.BlockSpec(memory_space=pl.ANY),
        scratch_shapes=[
            pltpu.VMEM((insts, page_rows, head_dim), arrived.dtype),
            pltpu.SemaphoreType.DMA((8,)),
        ],
        compiler_params=pltpu.CompilerParams(vmem_limit_bytes=4 * MIB),
        name="lend",
    )(arrived)


def join(arrived_ref, own_ref, out_ref, own, own_sem):
    query_count, head_dim = out_ref.shape
    first_row = arrived_ref.shape[1] - query_count - STAT_ROWS
    own_copy = pltpu.make_async_copy(own_ref, own, own_sem)
    own_copy.start()
    outs = arrived_ref[:, first_row : first_row + query_count].astype(jnp.float32)
    terms = arrived_ref[:, first_row + query_count :].astype(jnp.float32)[:, 0:1]
    shape = (query_count, head_dim)
    lane = lax.broadcasted_iota(jnp.int32, shape, 1)
    own_lane = (lane % query_count == lax.broadcasted_iota(jnp.int32, shape, 0)) & (lane < 3 * query_count)
    levels = jnp.sum(jnp.where(own_lane[None], terms, 0.0), axis=2, keepdims=True)
    own_copy.wait()
    own_mix, own_total, own_top = own[0], own[1], own[2]
    joint = jnp.maximum(jnp.max(levels, axis=0), own_top)
    factor = jnp.exp(levels - joint[None])
    own_factor = jnp.exp(own_top - joint)
    norm = jnp.sum(factor, axis=0) + own_total * own_factor
    mixture = jnp.sum(outs * factor, axis=0) + own_mix * own_factor
    out_ref[...] = (mixture / norm).astype(jnp.bfloat16)


def finish_kernel(arrived_ref, own_ref, out_ref, lent_ref, own, own_sem, lent_sem):
    lent_copy = pltpu.make_async_copy(arrived_ref.at[:, pl.ds(0, lent_ref.shape[1])], lent_ref, lent_sem)
    lent_copy.start()
    join(arrived_ref, own_ref, out_ref, own, own_sem)
    lent_copy.wait()


def finish(arrived, own, page_rows):
    insts, head_dim = arrived.shape[0], arrived.shape[2]
    attended = jax.ShapeDtypeStruct(own.shape[1:], jnp.bfloat16)
    scratch = [pltpu.VMEM(own.shape, own.dtype), pltpu.SemaphoreType.DMA]
    in_place = pl.BlockSpec(memory_space=pl.ANY)
    if page_rows:
        attended = (attended, pltpu.HBM((insts, page_rows, head_dim), arrived.dtype))
        scratch.append(pltpu.SemaphoreType.DMA)
    return pl.pallas_call(
        finish_kernel if page_rows else join,
        out_shape=attended,
        in_specs=[pl.BlockSpec(memory_space=pltpu.VMEM), in_place],
        out_specs=(pl.BlockSpec(memory_space=pltpu.VMEM), in_place)
        if page_rows
        else pl.BlockSpec(memory_space=pltpu.VMEM),
        scratch_shapes=scratch,
        compiler_params=pltpu.CompilerParams(vmem_limit_bytes=8 * MIB),
        name="finish" if page_rows else "join",
    )(in_vmem(arrived), in_hbm(own))


def shards(pool, sectioning, spill_to, tables, lengths, queries, new_kv):
    insts = lax.axis_size("inst")
    resident_slots, half_len, head_dim = pool.shape[0], pool.shape[3], pool.shape[4]
    sectioned = sectioning.shape[0]
    steps = queries.shape[1]
    query_count = steps * queries.shape[2]
    score_scale = head_dim ** (-0.5)
    query_rows = queries.reshape(query_count, head_dim)

    section_pages = sectioning.reshape(sectioned, 2 * half_len, head_dim)
    page_rows = CAP * 2 * half_len
    near_pool = pool.reshape(resident_slots, 2, half_len, head_dim)
    near_section = sectioning.reshape(sectioned, 2, half_len, head_dim)
    far_pool = lax.ppermute(near_pool, "core", [(0, 1), (1, 0)])
    far_section = lax.ppermute(near_section, "core", [(0, 1), (1, 0)])
    whole, paged, asking = pack(spill_to, section_pages, query_rows, insts)

    def exchange(outgoing):
        return lax.all_to_all(outgoing, "inst", split_axis=0, concat_axis=0, tiled=True)

    def owners():
        held_here = (tables[:, :, 0] == lax.axis_index("inst"))[:, :, None] & (
            tables[:, :, 1][:, :, None] == jnp.arange(resident_slots, dtype=jnp.int32)
        )
        request_ids = jnp.arange(tables.shape[0], dtype=jnp.int32)
        return jnp.sum(jnp.where(held_here, request_ids[:, None, None], 0), axis=(0, 1))

    def own_part(far_section):
        length = lax.dynamic_index_in_dim(lengths, lax.axis_index("inst"), 0, keepdims=False)
        place = jnp.stack([length, lax.axis_index("core").astype(jnp.int32)])
        fresh = lax.dynamic_slice_in_dim(new_kv[0], lax.axis_index("pair"), 1, 2)[:, :, 0]
        fresh = jnp.pad(jnp.swapaxes(fresh, 0, 1), ((0, 0), (0, query_count - steps), (0, 0)))
        return own_partial(place, query_rows, near_section, far_section, fresh, score_scale)

    def queries_first(whole, paged, asking, far_pool, far_section):
        asked = exchange(asking)
        own = own_part(far_section)
        paged = resident(owners(), asked, near_pool, far_pool, paged, score_scale, query_count)
        return finish(exchange(paged), own, page_rows)

    def pages_first(whole, paged, asking, far_pool, far_section):
        arrived = exchange(whole)
        own = own_part(far_section)
        partials = resident(owners(), arrived, near_pool, far_pool, None, score_scale, query_count)
        lent = lend(arrived, page_rows)
        return finish(exchange(partials), own, 0), lent

    attended, lent = lax.cond(
        lax.axis_index("core") == 0, queries_first, pages_first, whole, paged, asking, far_pool, far_section
    )
    return attended.reshape(queries.shape), lent.reshape(insts * CAP, 1, 2, half_len, head_dim)


def solution(mesh):
    insts, tp = mesh.devices.shape
    paired = Mesh(mesh.devices.reshape(insts, tp // 2, 2), ("inst", "pair", "core"))
    heads = ("pair", "core")
    return jax.shard_map(
        shards,
        mesh=paired,
        in_specs=(
            P("inst", heads),
            P("inst", heads),
            P("inst"),
            P(),
            P(),
            P("inst", None, heads),
            P("inst"),
        ),
        out_specs=(P("inst", None, heads), P("inst", heads)),
        check_vma=False,
    )
```
